256 devices in a mesh: seq: 32 (over z, x_hi, core), head: 8 (over x_lo, y).
Axes of the slice: x: 4 (x_hi: 2, x_lo: 2; x = x_hi * 2 + x_lo), y: 4, z: 8, core: 2. Of those that a mesh axis runs over, the one named last changes fastest.
Arguments:
- q_one: bfloat16 [4096, 2048], P('seq', 'head'), may hold values from -6 to 6
- q_two: bfloat16 [4096, 2048], P('seq', 'head'), may hold values from -6 to 6
- k_one: bfloat16 [4096, 2048], P('seq', 'head'), may hold values from -6 to 6
- k_two: bfloat16 [4096, 2048], P('seq', 'head'), may hold values from -6 to 6
- values: bfloat16 [4096, 4096], P('seq', 'head'), may hold values from -6 to 6
- out_grad: bfloat16 [4096, 4096], P('seq', 'head'), may hold values from -6 to 6
- lse_one: float32 [16, 4096], P('head', 'seq'), may hold values from 4 to 7
- lse_two: float32 [16, 4096], P('head', 'seq'), may hold values from 4 to 7
- delta_one: float32 [16, 4096], P('head', 'seq'), may hold values from -3 to 3
- delta_two: float32 [16, 4096], P('head', 'seq'), may hold values from -3 to 3
- doc_start: int32 [4096], replicated, may hold values from 0 to 4095, as said below
- skip_pairs: int32 [32, 32], replicated, may hold values from 0 to 1, as said below
- lambda_q1: float32 [128], replicated, may hold values from -0.5 to 0.5
- lambda_k1: float32 [128], replicated, may hold values from -0.5 to 0.5
- lambda_q2: float32 [128], replicated, may hold values from -0.5 to 0.5
- lambda_k2: float32 [128], replicated, may hold values from -0.5 to 0.5
Outputs:
- dq_one: bfloat16 [4096, 2048], P('seq', 'head')
- dq_two: bfloat16 [4096, 2048], P('seq', 'head')
- dk_one: bfloat16 [4096, 2048], P('seq', 'head')
- dk_two: bfloat16 [4096, 2048], P('seq', 'head')
- dv_out: bfloat16 [4096, 4096], P('seq', 'head')
- lambda_grads: float32 [4, 128], replicated
The draws below stay inside these ranges and needn't reach their ends.
Inputs may be any that keep to these rules, and one draw needn't show every extreme that they name: doc_start of a row is the position of the first token of its document: never above the row's own position, equal for all rows of one document; at position 0 it is 0, and the last position of the sequence starts a document of its own. skip_pairs[s, d] is 1 exactly when no query row held by seq index (d - s) mod the seq size sees any key row held by seq index d under the document and causal rule; row s = 0 is all zero.
All inputs are finite; a program needn't handle non-finite values.
Results may differ from the reference program's by a relative error of at most 0.0072.
Values may be sent and summed in bfloat16 or wider, within the bound.
A program may use at most 64 MiB of HBM per device.

```python
import math
import jax
import jax.numpy as jnp
from jax import lax

DK = 128
DV = 256
HEADS = 16
TOK_DEV = 128
TOKENS = 4096
N_SEQ = 32


def row_places():
    rows_all = jnp.arange(TOKENS, dtype=jnp.int32)
    device = rows_all // TOK_DEV
    within = rows_all % TOK_DEV
    half_rows = TOK_DEV // 2
    block_index = jnp.where(within < half_rows, device, 2 * N_SEQ - 1 - device)
    return (block_index * half_rows + within % half_rows).astype(jnp.int32)


def document_rows(key):
    positions = jnp.arange(TOKENS, dtype=jnp.int32)
    marks = jax.random.randint(key, (TOKENS,), 0, TOKENS) < 8
    marks = marks | (positions == 0) | (positions == TOKENS - 1)
    begins = lax.cummax(jnp.where(marks, positions, 0), axis=0)
    places = row_places()
    return (begins[places], places)


def draw_doc_start(key, part):
    starts, places = document_rows(key)
    return starts.astype(jnp.int32)


def draw_skip_pairs(key, part):
    starts, places = document_rows(key)
    half_rows = TOK_DEV // 2
    devices = jnp.arange(N_SEQ, dtype=jnp.int32)
    lowest = jnp.stack([devices * half_rows, (2 * N_SEQ - 1 - devices) * half_rows])
    highest = lowest + half_rows - 1
    reached = (starts[:, None, None] <= highest[None]) & (places[:, None, None] >= lowest[None])
    seen = jnp.any(reached, axis=1)
    paired = jnp.any(seen.reshape(N_SEQ, TOK_DEV, N_SEQ), axis=1)
    sources = (devices[None, :] - devices[:, None]) % N_SEQ
    table = paired[sources, jnp.broadcast_to(devices[None, :], (N_SEQ, N_SEQ))]
    return jnp.where(table, 0, 1).astype(jnp.int32)


def steps_of(key, dims, pieces, smallest, largest):
    gain, own = 1.0, jax.random.fold_in(key, 6)
    for position, blocks in pieces:
        steps = jnp.exp(jax.random.uniform(jax.random.fold_in(own, position), (blocks,), jnp.float32, smallest / len(pieces), largest / len(pieces)))
        gain = gain * jnp.repeat(steps, dims[position] // blocks).reshape([-1 if axis == position else 1 for axis in range(len(dims))])
    return gain


def scatter_about(rng, shape, spread, bound, cuts=(), kind=jnp.bfloat16):
    level = steps_of(rng, shape, cuts, -0.22, 0.18) if cuts else 1.0
    values = jax.random.normal(rng, shape, jnp.float32) * spread * level
    return jnp.minimum(jnp.maximum(values, -bound), bound).astype(kind)


def setup_inputs(seed: int = 0) -> dict:
    seeds = jax.random.split(jax.random.key(seed), 17)
    q_one = scatter_about(seeds[0], (TOKENS, HEADS * DK), 1.0, 6.0, ((0, 32), (1, 8)))
    q_two = scatter_about(seeds[1], (TOKENS, HEADS * DK), 1.0, 6.0, ((0, 32), (1, 8)))
    k_one = scatter_about(seeds[2], (TOKENS, HEADS * DK), 1.0, 6.0, ((0, 32), (1, 8)))
    k_two = scatter_about(seeds[3], (TOKENS, HEADS * DK), 1.0, 6.0, ((0, 32), (1, 8)))
    values = scatter_about(seeds[4], (TOKENS, HEADS * DV), 1.0, 6.0, ((0, 32), (1, 8)))
    out_grad = scatter_about(seeds[5], (TOKENS, HEADS * DV), 1.0, 6.0, ((0, 32), (1, 8)))
    lse_one = jnp.clip(4.0 + 3.0 * jax.random.uniform(seeds[6], (HEADS, TOKENS), jnp.float32) ** steps_of(seeds[6], (HEADS, TOKENS), ((0, 8), (1, 32)), -0.2, 0.2), 4.0, 7.0)
    lse_two = jnp.clip(4.0 + 3.0 * jax.random.uniform(seeds[7], (HEADS, TOKENS), jnp.float32) ** steps_of(seeds[7], (HEADS, TOKENS), ((0, 8), (1, 32)), -0.2, 0.2), 4.0, 7.0)
    delta_one = scatter_about(seeds[8], (HEADS, TOKENS), 0.5, 3.0, ((0, 8), (1, 32)), jnp.float32)
    delta_two = scatter_about(seeds[9], (HEADS, TOKENS), 0.5, 3.0, ((0, 8), (1, 32)), jnp.float32)
    doc_start = draw_doc_start(jax.random.fold_in(seeds[16], 71), 0)
    skip_pairs = draw_skip_pairs(jax.random.fold_in(seeds[16], 71), 0)
    lambda_q1 = scatter_about(seeds[12], (DK,), 0.1, 0.5, (), jnp.float32)
    lambda_k1 = scatter_about(seeds[13], (DK,), 0.1, 0.5, (), jnp.float32)
    lambda_q2 = scatter_about(seeds[14], (DK,), 0.1, 0.5, (), jnp.float32)
    lambda_k2 = scatter_about(seeds[15], (DK,), 0.1, 0.5, (), jnp.float32)
    return dict(q_one=q_one, q_two=q_two, k_one=k_one, k_two=k_two, values=values, out_grad=out_grad, lse_one=lse_one, lse_two=lse_two, delta_one=delta_one, delta_two=delta_two, doc_start=doc_start, skip_pairs=skip_pairs, lambda_q1=lambda_q1, lambda_k1=lambda_k1, lambda_q2=lambda_q2, lambda_k2=lambda_k2)


lambda_init = 0.8 - 0.6 * math.exp(-3.6)


def token_places():
    rows_all = jnp.arange(TOKENS, dtype=jnp.int32)
    device = rows_all // TOK_DEV
    within = rows_all % TOK_DEV
    half_rows = TOK_DEV // 2
    block_index = jnp.where(within < half_rows, device, 2 * N_SEQ - 1 - device)
    return (block_index * half_rows + within % half_rows).astype(jnp.int32)


def split_heads(array, head_width):
    return array.reshape(TOKENS, HEADS, head_width).transpose(1, 0, 2)


def join_heads(array, head_width):
    return array.transpose(1, 0, 2).reshape(TOKENS, HEADS * head_width)


def reference(q_one, q_two, k_one, k_two, values, out_grad, lse_one, lse_two, delta_one, delta_two, doc_start, skip_pairs, lambda_q1, lambda_k1, lambda_q2, lambda_k2):
    expo_one = jnp.exp(jnp.sum(lambda_q1 * lambda_k1))
    expo_two = jnp.exp(jnp.sum(lambda_q2 * lambda_k2))
    mixing = expo_one - expo_two + lambda_init
    places = token_places()
    hosts = jnp.arange(TOKENS, dtype=jnp.int32) // TOK_DEV
    score_scale = DK ** -0.5

    def per_head(operands):
        query_one, query_two, key_one, key_two, value_head, grad_head, lse_a, lse_b, delta_a, delta_b = operands

        def step_block(carry, source):
            dk_a, dk_b, dv_acc, lambda_acc = carry
            row_start = (source * TOK_DEV).astype(jnp.int32)
            query_a = lax.dynamic_slice_in_dim(query_one, row_start, TOK_DEV, 0)
            query_b = lax.dynamic_slice_in_dim(query_two, row_start, TOK_DEV, 0)
            grad_rows = lax.dynamic_slice_in_dim(grad_head, row_start, TOK_DEV, 0)
            lse_rows_a = lax.dynamic_slice_in_dim(lse_a, row_start, TOK_DEV, 0)
            lse_rows_b = lax.dynamic_slice_in_dim(lse_b, row_start, TOK_DEV, 0)
            delta_rows_a = lax.dynamic_slice_in_dim(delta_a, row_start, TOK_DEV, 0)
            delta_rows_b = lax.dynamic_slice_in_dim(delta_b, row_start, TOK_DEV, 0)
            query_places = lax.dynamic_slice_in_dim(places, row_start, TOK_DEV, 0)
            query_starts = lax.dynamic_slice_in_dim(doc_start, row_start, TOK_DEV, 0)
            hop_index = ((hosts - source) % N_SEQ).astype(jnp.int32)
            skipped = skip_pairs[hop_index, hosts]
            visible = (query_starts[:, None] <= places[None, :]) & (places[None, :] <= query_places[:, None]) & (skipped[None, :] == 0)
            score_one = jnp.dot(query_a, key_one.T, preferred_element_type=jnp.float32) * score_scale
            score_two = jnp.dot(query_b, key_two.T, preferred_element_type=jnp.float32) * score_scale
            prob_one = jnp.where(visible, jnp.exp(score_one - lse_rows_a[:, None]), 0.0)
            prob_two = jnp.where(visible, jnp.exp(score_two - lse_rows_b[:, None]), 0.0)
            inner_dot = jnp.dot(grad_rows, value_head.T, preferred_element_type=jnp.float32)
            dscore_one = (prob_one * (inner_dot - delta_rows_a[:, None])).astype(jnp.bfloat16)
            dscore_two = (prob_two * (-mixing * inner_dot - delta_rows_b[:, None])).astype(jnp.bfloat16)
            mixed_probs = (prob_one - mixing * prob_two).astype(jnp.bfloat16)
            dq_a = (jnp.dot(dscore_one, key_one, preferred_element_type=jnp.float32) * score_scale).astype(jnp.bfloat16)
            dq_b = (jnp.dot(dscore_two, key_two, preferred_element_type=jnp.float32) * score_scale).astype(jnp.bfloat16)
            dk_a = dk_a + jnp.dot(dscore_one.T, query_a, preferred_element_type=jnp.float32) * score_scale
            dk_b = dk_b + jnp.dot(dscore_two.T, query_b, preferred_element_type=jnp.float32) * score_scale
            dv_acc = dv_acc + jnp.dot(mixed_probs.T, grad_rows, preferred_element_type=jnp.float32)
            lambda_acc = lambda_acc - jnp.sum(prob_two * inner_dot)
            return (dk_a, dk_b, dv_acc, lambda_acc), (dq_a, dq_b)

        initial = (jnp.zeros((TOKENS, DK), jnp.float32), jnp.zeros((TOKENS, DK), jnp.float32), jnp.zeros((TOKENS, DV), jnp.float32), jnp.zeros((), jnp.float32))
        carry, stacked = lax.scan(step_block, initial, jnp.arange(N_SEQ, dtype=jnp.int32))
        dk_a, dk_b, dv_acc, lambda_acc = carry
        return (stacked[0].reshape(TOKENS, DK), stacked[1].reshape(TOKENS, DK), dk_a.astype(jnp.bfloat16), dk_b.astype(jnp.bfloat16), dv_acc.astype(jnp.bfloat16), lambda_acc)

    results = lax.map(per_head, (split_heads(q_one, DK), split_heads(q_two, DK), split_heads(k_one, DK), split_heads(k_two, DK), split_heads(values, DV), split_heads(out_grad, DV), lse_one, lse_two, delta_one, delta_two))
    lambda_total = jnp.sum(results[5])
    lambda_grads = jnp.stack([lambda_total * expo_one * lambda_k1, lambda_total * expo_one * lambda_q1, -lambda_total * expo_two * lambda_k2, -lambda_total * expo_two * lambda_q2])
    return (join_heads(results[0], DK), join_heads(results[1], DK), join_heads(results[2], DK), join_heads(results[3], DK), join_heads(results[4], DV), lambda_grads)
```

```python
import math

import jax
import jax.numpy as jnp
from jax import lax
from jax.experimental import pallas as pl
from jax.experimental.pallas import tpu as pltpu
from jax.sharding import PartitionSpec as P

MESH = pl.DeviceIdType.MESH
LAMBDA_INIT = 0.8 - 0.6 * math.exp(-3.6)
F32 = jnp.float32
BF16 = jnp.bfloat16

DK = 128
DV = 256
HALF = 64
COLS = 2 * DK + DV
PLANE = 4
PLANES = 8
DEVICES = PLANE * PLANES
HEAD_DEVICES = 8
LAST = PLANES - 1
FAR = 8192


def nt_dot(a, b):
    return lax.dot_general(a, b, (((1,), (1,)), ((), ())), preferred_element_type=F32)


def tn_dot(a, b):
    return lax.dot_general(a, b, (((0,), (0,)), ((), ())), preferred_element_type=F32)


def nn_dot(a, b):
    return lax.dot_general(a, b, (((1,), (0,)), ((), ())), preferred_element_type=F32)


def kernel(
    q1_ref, q2_ref, go_ref, k1_ref, k2_ref, v_ref,
    lse1_ref, lse2_ref, del1_ref, del2_ref, starts_ref, skip_ref,
    lq1_ref, lk1_ref, lq2_ref, lk2_ref,
    dq1_out, dq2_out, dk1_out, dk2_out, dv_out, lam_out,
    qpay, spay, kpay, kbuf, qbuf, sbuf,
    dqp, dqs, dqr, loc_send, loc_recv, loc_own, fin,
    dkv, dkv_send, dkv_recv,
    lam_acc, lam_send, lam_z, lam_p, lam_h,
    q_send, q_recv, s_send, s_recv, q0_sem, s0_sem, k_send, k_recv,
    d_send, d_recv, f_send, f_recv, l_send, l_recv, o_send, o_recv,
    z_send, z_recv, p_send, p_recv, h_send, h_recv,
):
    me = lax.axis_index("seq")
    hme = lax.axis_index("head")
    z = me // PLANE
    t_me = lax.rem(me, PLANE)
    col = t_me // 2
    core = lax.rem(t_me, 2)
    other = 1 - core
    zdn = lax.rem(z + PLANES - 1, PLANES)
    zup = lax.rem(z + 1, PLANES)

    def dev(zz, cc, kk):
        return zz * PLANE + cc * 2 + kk

    peers = [dev(z, col, other), dev(z, 1 - col, core), dev(z, 1 - col, other)]
    peer_head = [other, core, other]
    peer_t = [2 * col + other, 2 * (1 - col) + core, 2 * (1 - col) + other]
    ring = [zdn, zup]

    def send(src, dst, s_sem, r_sem, seq):
        return pltpu.make_async_remote_copy(
            src_ref=src, dst_ref=dst, send_sem=s_sem, recv_sem=r_sem,
            device_id={"seq": seq}, device_id_type=MESH,
        )

    barrier = pltpu.get_barrier_semaphore()
    for p in peers:
        pl.semaphore_signal(barrier, inc=1, device_id={"seq": p}, device_id_type=MESH)
    for off in range(1, PLANES):
        zz = lax.rem(z + off, PLANES)
        pl.semaphore_signal(barrier, inc=1, device_id={"seq": dev(zz, col, core)}, device_id_type=MESH)
    for zz in ring:
        pl.semaphore_signal(barrier, inc=1, device_id={"seq": dev(zz, col, other)}, device_id_type=MESH)
    for off in range(1, HEAD_DEVICES):
        pl.semaphore_signal(
            barrier, inc=1, device_id={"head": lax.rem(hme + off, HEAD_DEVICES)}, device_id_type=MESH
        )

    for h in range(2):
        for half in range(2):
            rows = slice(half * HALF, (half + 1) * HALF)
            for pay, a, b, g in ((qpay, q1_ref, q2_ref, go_ref), (kpay, k1_ref, k2_ref, v_ref)):
                pay[h, half, :, 0:DK] = a[rows, h * DK:(h + 1) * DK]
                pay[h, half, :, DK:2 * DK] = b[rows, h * DK:(h + 1) * DK]
                pay[h, half, :, 2 * DK:COLS] = g[rows, h * DV:(h + 1) * DV]
        for i, ref in enumerate((lse1_ref, lse2_ref, del1_ref, del2_ref)):
            spay[h, i:i + 1, :] = ref[h:h + 1, :]
        spay[h, 4:8, :] = jnp.zeros((4, 128), F32)

    my_rows = pl.ds(pl.multiple_of(core * HALF, HALF), HALF)
    qbuf[0, :, my_rows, :] = qpay[core]
    sbuf[0, 0, core] = spay[core]
    kbuf[:, t_me] = kpay[core]

    pl.semaphore_wait(barrier, 3 + LAST + 2 + HEAD_DEVICES - 1)

    def first_copies():
        out = []
        for d in range(2):
            for i, (h, k) in enumerate(((core, core), (other, other))):
                to = dev(ring[d], col, k)
                out.append(send(qpay.at[h, d], qbuf.at[1, d, my_rows, :], q_send.at[0, d, i], q_recv.at[1, d], to))
                out.append(send(spay.at[h], sbuf.at[1, d, core], s_send.at[0, d, i], s_recv.at[1, d], to))
        return out

    def key_copies():
        return [
            send(kpay.at[peer_head[i]], kbuf.at[:, t_me], k_send.at[i], k_recv.at[i], peers[i]) for i in range(3)
        ]

    def pair_copies():
        return [
            send(qpay.at[other], qbuf.at[0, :, my_rows, :], q0_sem.at[0], q0_sem.at[1], peers[0]),
            send(spay.at[other], sbuf.at[0, 0, core], s0_sem.at[0], s0_sem.at[1], peers[0]),
        ]

    for cp in first_copies():
        cp.start()
    for cp in key_copies():
        cp.start()
    for cp in pair_copies():
        cp.start()

    e1 = jnp.exp(jnp.sum(lq1_ref[...] * lk1_ref[...], axis=1, keepdims=True))
    e2 = jnp.exp(jnp.sum(lq2_ref[...] * lk2_ref[...], axis=1, keepdims=True))
    mixing = e1 - e2 + LAMBDA_INIT
    scale = DK ** -0.5

    dkv[...] = jnp.zeros_like(dkv)
    lam_acc[...] = jnp.zeros_like(lam_acc)

    def hop_copies(j, d):
        to = dev(ring[d], col, core)
        return (
            send(qbuf.at[j, d], qbuf.at[j + 1, d], q_send.at[j, d, 0], q_recv.at[j + 1, d], to),
            send(sbuf.at[j, d], sbuf.at[j + 1, d], s_send.at[j, d, 0], s_recv.at[j + 1, d], to),
        )

    def dq_copy(j, d):
        return send(dqs.at[j, d], dqr.at[j + 1, d], d_send.at[j, d], d_recv.at[j + 1, d], dev(ring[d], col, core))

    def low_here(j):
        return z + j <= LAST

    def wait_block(j, d):
        pltpu.make_async_copy(qbuf.at[j, d], qbuf.at[j, d], q_recv.at[j, d]).wait()
        pltpu.make_async_copy(sbuf.at[j, d], sbuf.at[j, d], s_recv.at[j, d]).wait()

    lane = lax.broadcasted_iota(jnp.int32, (1, 2 * HALF), 1)
    first = lane < HALF
    sub = lax.broadcasted_iota(jnp.int32, (HALF, 1), 0)

    def merge(a, b, d):
        if d == 0:
            return jnp.where(first, a, pltpu.roll(b, HALF, 1))
        return jnp.where(first, pltpu.roll(a, HALF, 1), b)

    def tile(j, sd, d, zq, kh):
        stats = merge(sbuf[j, sd, 0], sbuf[j, sd, 1], d)
        lse_a, lse_b, del_a, del_b = (stats[i:i + 1] for i in range(4))
        host = PLANE * zq + 2 * col
        starts = merge(starts_ref[pl.ds(host, 1), :], starts_ref[pl.ds(host + 1, 1), :], d)
        if d == 0:
            qpos = host * HALF + lane
        else:
            qpos = jnp.where(first, (2 * DEVICES - 1 - host) * HALF + lane, (2 * DEVICES - 3 - host) * HALF + lane)
        seen = []
        for t in range(PLANE):
            khost = PLANE * z + t
            base = khost * HALF if kh == 0 else (2 * DEVICES - 1 - khost) * HALF
            skip_a = skip_ref[lax.rem(khost - host + DEVICES, DEVICES), khost]
            skip_b = skip_ref[lax.rem(khost - host - 1 + DEVICES, DEVICES), khost]
            start = starts - base + jnp.where(first, skip_a, skip_b) * FAR
            seen.append((sub >= start) & (sub <= qpos - base))
        visible = jnp.concatenate(seen, axis=0)
        qa = qbuf[j, d, :, 0:DK]
        qb = qbuf[j, d, :, DK:2 * DK]
        g = qbuf[j, d, :, 2 * DK:COLS]
        keys = kbuf[kh].reshape(PLANE * HALF, COLS)
        ka, kb, vals = keys[:, 0:DK], keys[:, DK:2 * DK], keys[:, 2 * DK:COLS]
        pa = jnp.where(visible, jnp.exp(nt_dot(ka, qa) * scale - lse_a), 0.0)
        pb = jnp.where(visible, jnp.exp(nt_dot(kb, qb) * scale - lse_b), 0.0)
        inner = nt_dot(vals, g)
        dsa = (pa * (inner - del_a)).astype(BF16)
        dsb = (pb * (-mixing * inner - del_b)).astype(BF16)
        mix = (pa - mixing * pb).astype(BF16)
        lam_acc[...] += jnp.sum((pb * inner).reshape(PLANE * HALF // 8, 8, 2 * HALF), axis=0)
        dkv[kh, :, 0:DK] += nn_dot(dsa, qa)
        dkv[kh, :, DK:2 * DK] += nn_dot(dsb, qb)
        dkv[kh, :, 2 * DK:COLS] += nn_dot(mix, g)
        dqp[d, :, 0:DK] += tn_dot(dsa, ka) * scale
        dqp[d, :, DK:2 * DK] += tn_dot(dsb, kb) * scale

    def home_copies(half):
        return [
            send(
                dkv_send.at[i, half], dkv_recv.at[i, half], o_send.at[i, half], o_recv.at[i, half], peers[i],
            )
            for i in range(3)
        ]

    def send_home(half):
        for i in range(3):
            rows = pl.ds(pl.multiple_of(peer_t[i] * HALF, HALF), HALF)
            dkv_send[i, half, :, 0:2 * DK] = (dkv[half, rows, 0:2 * DK] * scale).astype(BF16)
            dkv_send[i, half, :, 2 * DK:COLS] = dkv[half, rows, 2 * DK:COLS].astype(BF16)
        for cp in home_copies(half):
            cp.start()

    def work(j, d):
        dqp[d] = jnp.zeros((2 * HALF, 2 * DK), F32)
        if d == 0:
            @pl.when(low_here(j))
            def _():
                tile(j, 0, 0, z + j, 0)
        else:
            zq = lax.rem(z - j + PLANES, PLANES)
            tile(j, 1, 1, zq, 0)

            @pl.when(j <= z)
            def _():
                tile(j, 1, 1, zq, 1)

    def take_block(j):
        @pl.when(low_here(j))
        def _():
            wait_block(j, 0)

        wait_block(j, 1)

    def forward(j):
        @pl.when(low_here(j) & (z > 0))
        def _():
            for cp in hop_copies(j, 0):
                cp.start()

        for cp in hop_copies(j, 1):
            cp.start()

    wait_block(1, 0)
    wait_block(1, 1)
    forward(1)

    for cp in pair_copies():
        cp.wait()
    for cp in key_copies():
        cp.wait()
    for d in range(2):
        dqp[d] = jnp.zeros((2 * HALF, 2 * DK), F32)
    tile(0, 0, 0, z, 0)
    tile(0, 0, 1, z, 0)
    tile(0, 0, 1, z, 1)
    their_rows = pl.ds(pl.multiple_of(other * HALF, HALF), HALF)
    for d in range(2):
        loc_own[d] = dqp[d, my_rows, :]
        loc_send[d] = dqp[d, their_rows, :]
    loc_copy = send(loc_send, loc_recv, l_send, l_recv, peers[0])
    loc_copy.start()

    @pl.when(z == 0)
    def _():
        send_home(1)

    take_block(2)
    forward(2)
    for d in range(2):
        work(1, d)
        dqs[1, d] = dqp[d].astype(BF16)
        dq_copy(1, d).start()

    @pl.when(z == 1)
    def _():
        send_home(1)

    def step(j, carry):
        take_block(j + 1)

        @pl.when(j + 1 < LAST)
        def _():
            forward(j + 1)

        for d in range(2):
            work(j, d)
            pltpu.make_async_copy(dqr.at[j, d], dqr.at[j, d], d_recv.at[j, d]).wait()
            dqs[j, d] = (dqr[j, d].astype(F32) + dqp[d]).astype(BF16)
            dq_copy(j, d).start()

        @pl.when(j == z)
        def _():
            send_home(1)

        return carry

    lax.fori_loop(2, LAST, step, 0)

    def fin_copies(d):
        out = []
        for i, k in enumerate((core, other)):
            rows = pl.ds(pl.multiple_of(k * HALF, HALF), HALF)
            out.append(
                send(dqs.at[LAST, d, rows, :], fin.at[d, core], f_send.at[d, i], f_recv.at[d, i], dev(ring[d], col, k))
            )
        return out

    for d in range(2):
        work(LAST, d)
        pltpu.make_async_copy(dqr.at[LAST, d], dqr.at[LAST, d], d_recv.at[LAST, d]).wait()
        dqs[LAST, d] = (dqr[LAST, d].astype(F32) + dqp[d]).astype(BF16)
        for cp in fin_copies(d):
            cp.start()

    @pl.when(z == LAST)
    def _():
        send_home(1)

    send_home(0)

    lam_send[0] = lam_acc[...]
    z_copies = [
        send(lam_send.at[0], lam_z.at[off - 1], z_send.at[off - 1], z_recv.at[off - 1],
             dev(lax.rem(z + off, PLANES), col, core))
        for off in range(1, PLANES)
    ]
    for cp in z_copies:
        cp.start()
    for cp in z_copies:
        cp.wait()
    lam_send[1] = lam_send[0] + jnp.sum(lam_z[...], axis=0)
    p_copies = [send(lam_send.at[1], lam_p.at[i], p_send.at[i], p_recv.at[i], peers[i]) for i in range(3)]
    for cp in p_copies:
        cp.start()
    for cp in p_copies:
        cp.wait()
    lam_send[2] = lam_send[1] + jnp.sum(lam_p[...], axis=0)
    h_copies = [
        pltpu.make_async_remote_copy(
            src_ref=lam_send.at[2], dst_ref=lam_h.at[off - 1], send_sem=h_send.at[off - 1], recv_sem=h_recv.at[off - 1],
            device_id={"head": lax.rem(hme + off, HEAD_DEVICES)}, device_id_type=MESH,
        )
        for off in range(1, HEAD_DEVICES)
    ]
    for cp in h_copies:
        cp.start()

    loc_copy.wait()
    for d in range(2):
        for cp in fin_copies(d):
            cp.wait()
        rows = slice(d * HALF, (d + 1) * HALF)
        mine = loc_own[d] + fin[d, core].astype(F32)
        theirs = loc_recv[d] + fin[d, other].astype(F32)
        for h in range(2):
            val = jnp.where(core == h, mine, theirs).astype(BF16)
            dq1_out[rows, h * DK:(h + 1) * DK] = val[:, 0:DK]
            dq2_out[rows, h * DK:(h + 1) * DK] = val[:, DK:2 * DK]

    key_rows = pl.ds(pl.multiple_of(t_me * HALF, HALF), HALF)
    for half in (1, 0):
        for cp in home_copies(half):
            cp.wait()
        rows = slice(half * HALF, (half + 1) * HALF)
        own = dkv[half, key_rows, :]
        mine_k = own[:, 0:2 * DK] * scale + dkv_recv[1, half, :, 0:2 * DK].astype(F32)
        mine_v = own[:, 2 * DK:COLS] + dkv_recv[1, half, :, 2 * DK:COLS].astype(F32)
        theirs = dkv_recv[0, half].astype(F32) + dkv_recv[2, half].astype(F32)
        for h in range(2):
            val_k = jnp.where(core == h, mine_k, theirs[:, 0:2 * DK]).astype(BF16)
            val_v = jnp.where(core == h, mine_v, theirs[:, 2 * DK:COLS]).astype(BF16)
            dk1_out[rows, h * DK:(h + 1) * DK] = val_k[:, 0:DK]
            dk2_out[rows, h * DK:(h + 1) * DK] = val_k[:, DK:2 * DK]
            dv_out[rows, h * DV:(h + 1) * DV] = val_v

    for cp in h_copies:
        cp.wait()
    total_tile = lam_send[2] + jnp.sum(lam_h[...], axis=0)
    total = -jnp.sum(jnp.sum(total_tile, axis=0, keepdims=True), axis=1, keepdims=True)
    lam_out[0:1, :] = total * e1 * lk1_ref[...]
    lam_out[1:2, :] = total * e1 * lq1_ref[...]
    lam_out[2:3, :] = -total * e2 * lk2_ref[...]
    lam_out[3:4, :] = -total * e2 * lq2_ref[...]

    for cp in first_copies():
        cp.wait_send()
    for j in range(1, LAST):
        @pl.when(low_here(j) & (z > 0))
        def _():
            for cp in hop_copies(j, 0):
                cp.wait_send()

        for cp in hop_copies(j, 1):
            cp.wait_send()
        for d in range(2):
            dq_copy(j, d).wait_send()


def fused(*args):
    (q1, q2, k1, k2, v, go, lse1, lse2, d1, d2, starts, skip, lq1, lk1, lq2, lk2) = args
    rows = q1.shape[0]
    vm = pl.BlockSpec(memory_space=pltpu.VMEM)
    dma = pltpu.SemaphoreType.DMA
    lam_tile = (8, 2 * HALF)
    scratch = [
        pltpu.VMEM((2, 2, HALF, COLS), BF16),
        pltpu.VMEM((2, 8, 2 * HALF), F32),
        pltpu.VMEM((2, 2, HALF, COLS), BF16),
        pltpu.VMEM((2, PLANE, HALF, COLS), BF16),
        pltpu.VMEM((PLANES, 2, 2 * HALF, COLS), BF16),
        pltpu.VMEM((PLANES, 2, 2, 8, 2 * HALF), F32),
        pltpu.VMEM((2, 2 * HALF, 2 * DK), F32),
        pltpu.VMEM((PLANES, 2, 2 * HALF, 2 * DK), BF16),
        pltpu.VMEM((PLANES, 2, 2 * HALF, 2 * DK), BF16),
        pltpu.VMEM((2, HALF, 2 * DK), F32),
        pltpu.VMEM((2, HALF, 2 * DK), F32),
        pltpu.VMEM((2, HALF, 2 * DK), F32),
        pltpu.VMEM((2, 2, HALF, 2 * DK), BF16),
        pltpu.VMEM((2, PLANE * HALF, COLS), F32),
        pltpu.VMEM((3, 2, HALF, COLS), BF16),
        pltpu.VMEM((3, 2, HALF, COLS), BF16),
        pltpu.VMEM(lam_tile, F32),
        pltpu.VMEM((3,) + lam_tile, F32),
        pltpu.VMEM((LAST,) + lam_tile, F32),
        pltpu.VMEM((3,) + lam_tile, F32),
        pltpu.VMEM((HEAD_DEVICES - 1,) + lam_tile, F32),
        dma((PLANES, 2, 2)), dma((PLANES, 2)),
        dma((PLANES, 2, 2)), dma((PLANES, 2)),
        dma((2,)), dma((2,)),
        dma((3,)), dma((3,)),
        dma((PLANES, 2)), dma((PLANES, 2)),
        dma((2, 2)), dma((2, 2)),
        dma, dma,
        dma((3, 2)), dma((3, 2)),
        dma((LAST,)), dma((LAST,)),
        dma((3,)), dma((3,)),
        dma((HEAD_DEVICES - 1,)), dma((HEAD_DEVICES - 1,)),
    ]
    outs = [jax.ShapeDtypeStruct(a.shape, BF16) for a in (q1, q2, k1, k2, v)]
    outs.append(jax.ShapeDtypeStruct((4, DK), F32))
    row = lambda a: a.reshape(1, DK)
    return pl.pallas_call(
        kernel,
        out_shape=outs,
        in_specs=[vm] * 11 + [pl.BlockSpec(memory_space=pltpu.SMEM)] + [vm] * 4,
        out_specs=[vm] * 6,
        scratch_shapes=scratch,
        compiler_params=pltpu.CompilerParams(
            collective_id=0, has_side_effects=True, vmem_limit_bytes=32 * 1024 * 1024
        ),
    )(
        q1, q2, go, k1, k2, v, lse1, lse2, d1, d2, starts.reshape(DEVICES, rows), skip,
        row(lq1), row(lk1), row(lq2), row(lk2),
    )


def solution(mesh):
    tok = P("seq", "head")
    stat = P("head", "seq")
    return jax.shard_map(
        fused,
        mesh=mesh,
        in_specs=(tok,) * 6 + (stat,) * 4 + (P(),) * 6,
        out_specs=(tok,) * 5 + (P(),),
        check_vma=False,
    )
```

```python
import math

import jax
import jax.numpy as jnp
from jax import lax
from jax.experimental import pallas as pl
from jax.experimental.pallas import tpu as pltpu
from jax.sharding import PartitionSpec as P

MESH = pl.DeviceIdType.MESH
LAMBDA_INIT = 0.8 - 0.6 * math.exp(-3.6)
F32 = jnp.float32
BF16 = jnp.bfloat16

DK = 128
DV = 256
HALF = 64
COLS = 2 * DK + DV
PLANE = 4
PLANES = 8
DEVICES = PLANE * PLANES
HEAD_DEVICES = 8
LAST = PLANES - 1
FAR = 8192
VMEM_LIMIT = 60 * 1024 * 1024


def nt_dot(a, b):
    return lax.dot_general(a, b, (((1,), (1,)), ((), ())), preferred_element_type=F32)


def tn_dot(a, b):
    return lax.dot_general(a, b, (((0,), (0,)), ((), ())), preferred_element_type=F32)


def nn_dot(a, b):
    return lax.dot_general(a, b, (((1,), (0,)), ((), ())), preferred_element_type=F32)


def kernel(
    q1_ref, q2_ref, go_ref, k1_ref, k2_ref, v_ref,
    lse1_ref, lse2_ref, del1_ref, del2_ref, starts_ref, skip_ref,
    lq1_ref, lk1_ref, lq2_ref, lk2_ref,
    dq1_out, dq2_out, dk1_out, dk2_out, dv_out, lam_out,
    qpay, spay, kpay, kbuf, qbuf, sbuf,
    dqp, dqs, dqr, loc_send, loc_recv, loc_own, fin,
    dkv, dkv_send, dkv_recv,
    lam_acc, lam_send, lam_z, lam_p, lam_h,
    in_sem, q_send, q_recv, s_send, s_recv, q0_sem, s0_sem, k_send, k_recv,
    d_send, d_recv, f_send, f_recv, l_send, l_recv, o_send, o_recv,
    z_send, z_recv, p_send, p_recv, h_send, h_recv,
):
    me = lax.axis_index("seq")
    hme = lax.axis_index("head")
    z = me // PLANE
    t_me = lax.rem(me, PLANE)
    col = t_me // 2
    core = lax.rem(t_me, 2)
    other = 1 - core
    zdn = lax.rem(z + PLANES - 1, PLANES)
    zup = lax.rem(z + 1, PLANES)

    def dev(zz, cc, kk):
        return zz * PLANE + cc * 2 + kk

    peers = [dev(z, col, other), dev(z, 1 - col, core), dev(z, 1 - col, other)]
    peer_head = [other, core, other]
    peer_t = [2 * col + other, 2 * (1 - col) + core, 2 * (1 - col) + other]
    ring = [zdn, zup]

    def send(src, dst, s_sem, r_sem, seq):
        return pltpu.make_async_remote_copy(
            src_ref=src, dst_ref=dst, send_sem=s_sem, recv_sem=r_sem,
            device_id={"seq": seq}, device_id_type=MESH,
        )

    barrier = pltpu.get_barrier_semaphore()
    for p in peers:
        pl.semaphore_signal(barrier, inc=1, device_id={"seq": p}, device_id_type=MESH)
    for off in range(1, PLANES):
        zz = lax.rem(z + off, PLANES)
        pl.semaphore_signal(barrier, inc=1, device_id={"seq": dev(zz, col, core)}, device_id_type=MESH)
    for zz in ring:
        pl.semaphore_signal(barrier, inc=1, device_id={"seq": dev(zz, col, other)}, device_id_type=MESH)
    for off in range(1, HEAD_DEVICES):
        pl.semaphore_signal(
            barrier, inc=1, device_id={"head": lax.rem(hme + off, HEAD_DEVICES)}, device_id_type=MESH
        )

    packs = []
    for n, (pay, parts) in enumerate(((qpay, (q1_ref, q2_ref, go_ref)), (kpay, (k1_ref, k2_ref, v_ref)))):
        for h in range(2):
            for i, (ref, at, width) in enumerate(zip(parts, (0, DK, 2 * DK), (DK, DK, DV))):
                cp = pltpu.make_async_copy(
                    ref.at[:, h * width:(h + 1) * width], pay.at[h, :, at:at + width], in_sem.at[n, h, i]
                )
                cp.start()
                packs.append(cp)
    for h in range(2):
        for i, ref in enumerate((lse1_ref, lse2_ref, del1_ref, del2_ref)):
            spay[h, i:i + 1, :] = ref[h:h + 1, :]
        spay[h, 4:8, :] = jnp.zeros((4, 128), F32)

    my_rows = pl.ds(pl.multiple_of(core * HALF, HALF), HALF)
    for cp in packs:
        cp.wait()

    pl.semaphore_wait(barrier, 3 + LAST + 2 + HEAD_DEVICES - 1)

    def first_copies():
        out = []
        for d in range(2):
            for i, (h, k) in enumerate(((core, core), (other, other))):
                to = dev(ring[d], col, k)
                out.append(send(
                    qpay.at[h, d * HALF:(d + 1) * HALF], qbuf.at[1, d, my_rows, :], q_send.at[0, d, i],
                    q_recv.at[1, d, core], to))
                out.append(send(spay.at[h], sbuf.at[1, d, core], s_send.at[0, d, i], s_recv.at[1, d], to))
        return out

    def key_copies():
        return [
            send(kpay.at[peer_head[i], half * HALF:(half + 1) * HALF], kbuf.at[half, t_me], k_send.at[i, half],
                 k_recv.at[i, half], peers[i])
            for half in range(2) for i in range(3)
        ]

    def pair_copies():
        return [
            send(qpay.at[other, 0:HALF], qbuf.at[0, 0, my_rows, :], q0_sem.at[0], q0_sem.at[1], peers[0]),
            send(qpay.at[other, HALF:2 * HALF], qbuf.at[0, 1, my_rows, :], q0_sem.at[2], q0_sem.at[3], peers[0]),
            send(spay.at[other], sbuf.at[0, 0, core], s0_sem.at[0], s0_sem.at[1], peers[0]),
        ]

    for cp in key_copies():
        cp.start()
    for cp in first_copies():
        cp.start()
    for cp in pair_copies():
        cp.start()

    sbuf[0, 0, core] = spay[core]
    for half in range(2):
        qbuf[0, half, my_rows, :] = qpay[core, half * HALF:(half + 1) * HALF]
        kbuf[half, t_me] = kpay[core, half * HALF:(half + 1) * HALF]

    e1 = jnp.exp(jnp.sum(lq1_ref[...] * lk1_ref[...], axis=1, keepdims=True))
    e2 = jnp.exp(jnp.sum(lq2_ref[...] * lk2_ref[...], axis=1, keepdims=True))
    mixing = e1 - e2 + LAMBDA_INIT
    scale = DK ** -0.5

    dkv[...] = jnp.zeros_like(dkv)
    lam_acc[...] = jnp.zeros_like(lam_acc)

    def piece(i):
        return slice(i * HALF, (i + 1) * HALF)

    def hop_copies(j, d, i):
        to = dev(ring[d], col, core)
        out = [send(qbuf.at[j, d, piece(i)], qbuf.at[j + 1, d, piece(i)], q_send.at[j, d, i], q_recv.at[j + 1, d, i], to)]
        if i == 1:
            out.append(send(sbuf.at[j, d], sbuf.at[j + 1, d], s_send.at[j, d, 0], s_recv.at[j + 1, d], to))
        return out

    def dq_copy(j, d, i):
        return send(dqs.at[j, d, piece(i)], dqr.at[j + 1, d, piece(i)], d_send.at[j, d, i], d_recv.at[j + 1, d, i],
                    dev(ring[d], col, core))

    def low_here(j):
        return z + j <= LAST

    def wait_piece(j, d, i):
        block = qbuf.at[j, d, piece(i)]
        pltpu.make_async_copy(block, block, q_recv.at[j, d, i]).wait()
        if i == 1:
            pltpu.make_async_copy(sbuf.at[j, d], sbuf.at[j, d], s_recv.at[j, d]).wait()

    lane = lax.broadcasted_iota(jnp.int32, (1, 2 * HALF), 1)
    first = lane < HALF
    sub = lax.broadcasted_iota(jnp.int32, (HALF, 1), 0)

    def merge(a, b, d):
        if d == 0:
            return jnp.where(first, a, pltpu.roll(b, HALF, 1))
        return jnp.where(first, pltpu.roll(a, HALF, 1), b)

    def tile(j, sd, d, zq, kh):
        stats = merge(sbuf[j, sd, 0], sbuf[j, sd, 1], d)
        lse_a, lse_b, del_a, del_b = (stats[i:i + 1] for i in range(4))
        host = PLANE * zq + 2 * col
        starts = merge(starts_ref[pl.ds(host, 1), :], starts_ref[pl.ds(host + 1, 1), :], d)
        if d == 0:
            qpos = host * HALF + lane
        else:
            qpos = jnp.where(first, (2 * DEVICES - 1 - host) * HALF + lane, (2 * DEVICES - 3 - host) * HALF + lane)
        seen = []
        for t in range(PLANE):
            khost = PLANE * z + t
            base = khost * HALF if kh == 0 else (2 * DEVICES - 1 - khost) * HALF
            skip_a = skip_ref[lax.rem(khost - host + DEVICES, DEVICES), khost]
            skip_b = skip_ref[lax.rem(khost - host - 1 + DEVICES, DEVICES), khost]
            start = starts - base + jnp.where(first, skip_a, skip_b) * FAR
            seen.append((sub >= start) & (sub <= qpos - base))
        visible = jnp.concatenate(seen, axis=0)
        qa = qbuf[j, d, :, 0:DK]
        qb = qbuf[j, d, :, DK:2 * DK]
        g = qbuf[j, d, :, 2 * DK:COLS]
        keys = kbuf[kh].reshape(PLANE * HALF, COLS)
        ka, kb, vals = keys[:, 0:DK], keys[:, DK:2 * DK], keys[:, 2 * DK:COLS]
        pa = jnp.where(visible, jnp.exp(nt_dot(ka, qa) * scale - lse_a), 0.0)
        pb = jnp.where(visible, jnp.exp(nt_dot(kb, qb) * scale - lse_b), 0.0)
        inner = nt_dot(vals, g)
        dsa = (pa * (inner - del_a)).astype(BF16)
        dsb = (pb * (-mixing * inner - del_b)).astype(BF16)
        mix = (pa - mixing * pb).astype(BF16)
        lam_acc[...] += jnp.sum((pb * inner).reshape(PLANE * HALF // 8, 8, 2 * HALF), axis=0)
        dkv[kh, :, 0:DK] += nn_dot(dsa, qa)
        dkv[kh, :, DK:2 * DK] += nn_dot(dsb, qb)
        dkv[kh, :, 2 * DK:COLS] += nn_dot(mix, g)
        dqp[d, :, 0:DK] += tn_dot(dsa, ka) * scale
        dqp[d, :, DK:2 * DK] += tn_dot(dsb, kb) * scale

    def home_copies(half):
        return [
            send(
                dkv_send.at[i, half], dkv_recv.at[i, half], o_send.at[i, half], o_recv.at[i, half], peers[i],
            )
            for i in range(3)
        ]

    def send_home(half):
        for i in range(3):
            rows = pl.ds(pl.multiple_of(peer_t[i] * HALF, HALF), HALF)
            dkv_send[i, half, :, 0:2 * DK] = (dkv[half, rows, 0:2 * DK] * scale).astype(BF16)
            dkv_send[i, half, :, 2 * DK:COLS] = dkv[half, rows, 2 * DK:COLS].astype(BF16)
        for cp in home_copies(half):
            cp.start()

    def work(j, d):
        dqp[d] = jnp.zeros((2 * HALF, 2 * DK), F32)
        if d == 0:
            @pl.when(low_here(j))
            def _():
                tile(j, 0, 0, z + j, 0)
        else:
            zq = lax.rem(z - j + PLANES, PLANES)
            tile(j, 1, 1, zq, 0)

            @pl.when(j <= z)
            def _():
                tile(j, 1, 1, zq, 1)

    def relay(j, i, last):
        @pl.when(low_here(j))
        def _():
            wait_piece(j, 0, i)

        if last is not True:
            @pl.when(low_here(j) & (z > 0) & jnp.logical_not(last))
            def _():
                for cp in hop_copies(j, 0, i):
                    cp.start()

        wait_piece(j, 1, i)
        if last is not True:
            @pl.when(jnp.logical_not(last))
            def _():
                for cp in hop_copies(j, 1, i):
                    cp.start()

    def pass_sums(j, d, first_hop):
        for i in range(2):
            part = dqp[d, piece(i)]
            if not first_hop:
                block = dqr.at[j, d, piece(i)]
                pltpu.make_async_copy(block, block, d_recv.at[j, d, i]).wait()
                part = part + dqr[j, d, piece(i)].astype(F32)
            dqs[j, d, piece(i)] = part.astype(BF16)
            if j is not LAST:
                dq_copy(j, d, i).start()

    for i in range(2):
        for d in range(2):
            wait_piece(1, d, i)

            @pl.when((d == 1) | (low_here(1) & (z > 0)))
            def _():
                for cp in hop_copies(1, d, i):
                    cp.start()

    for cp in pair_copies():
        cp.wait()
    for cp in key_copies():
        cp.wait()
    for d in range(2):
        dqp[d] = jnp.zeros((2 * HALF, 2 * DK), F32)
    tile(0, 0, 0, z, 0)
    tile(0, 0, 1, z, 0)
    tile(0, 0, 1, z, 1)
    their_rows = pl.ds(pl.multiple_of(other * HALF, HALF), HALF)
    for d in range(2):
        loc_own[d] = dqp[d, my_rows, :]
        loc_send[d] = dqp[d, their_rows, :]
    loc_copy = send(loc_send, loc_recv, l_send, l_recv, peers[0])
    loc_copy.start()

    @pl.when(z == 0)
    def _():
        send_home(1)

    for d in range(2):
        relay(2, d, False)
        work(1, d)
        pass_sums(1, d, True)

    @pl.when(z == 1)
    def _():
        send_home(1)

    def step(j, carry):
        for d in range(2):
            relay(j + 1, d, j + 1 == LAST)
            work(j, d)
            pass_sums(j, d, False)

        @pl.when(j == z)
        def _():
            send_home(1)

        return carry

    lax.fori_loop(2, LAST, step, 0)

    def fin_copies(d):
        out = []
        for i, k in enumerate((core, other)):
            rows = pl.ds(pl.multiple_of(k * HALF, HALF), HALF)
            out.append(
                send(dqs.at[LAST, d, rows, :], fin.at[d, core], f_send.at[d, i], f_recv.at[d, i], dev(ring[d], col, k))
            )
        return out

    for d in range(2):
        work(LAST, d)
        pass_sums(LAST, d, False)
        for cp in fin_copies(d):
            cp.start()

    @pl.when(z == LAST)
    def _():
        send_home(1)

    send_home(0)

    lam_send[0] = lam_acc[...]
    z_copies = [
        send(lam_send.at[0], lam_z.at[off - 1], z_send.at[off - 1], z_recv.at[off - 1],
             dev(lax.rem(z + off, PLANES), col, core))
        for off in range(1, PLANES)
    ]
    for cp in z_copies:
        cp.start()
    for cp in z_copies:
        cp.wait()
    lam_send[1] = lam_send[0] + jnp.sum(lam_z[...], axis=0)
    p_copies = [send(lam_send.at[1], lam_p.at[i], p_send.at[i], p_recv.at[i], peers[i]) for i in range(3)]
    for cp in p_copies:
        cp.start()
    for cp in p_copies:
        cp.wait()
    lam_send[2] = lam_send[1] + jnp.sum(lam_p[...], axis=0)
    h_copies = [
        pltpu.make_async_remote_copy(
            src_ref=lam_send.at[2], dst_ref=lam_h.at[off - 1], send_sem=h_send.at[off - 1], recv_sem=h_recv.at[off - 1],
            device_id={"head": lax.rem(hme + off, HEAD_DEVICES)}, device_id_type=MESH,
        )
        for off in range(1, HEAD_DEVICES)
    ]
    for cp in h_copies:
        cp.start()

    loc_copy.wait()
    for d in range(2):
        for cp in fin_copies(d):
            cp.wait()
        rows = slice(d * HALF, (d + 1) * HALF)
        mine = loc_own[d] + fin[d, core].astype(F32)
        theirs = loc_recv[d] + fin[d, other].astype(F32)
        for h in range(2):
            val = jnp.where(core == h, mine, theirs).astype(BF16)
            dq1_out[rows, h * DK:(h + 1) * DK] = val[:, 0:DK]
            dq2_out[rows, h * DK:(h + 1) * DK] = val[:, DK:2 * DK]

    key_rows = pl.ds(pl.multiple_of(t_me * HALF, HALF), HALF)
    for half in (1, 0):
        for cp in home_copies(half):
            cp.wait()
        rows = slice(half * HALF, (half + 1) * HALF)
        own = dkv[half, key_rows, :]
        mine_k = own[:, 0:2 * DK] * scale + dkv_recv[1, half, :, 0:2 * DK].astype(F32)
        mine_v = own[:, 2 * DK:COLS] + dkv_recv[1, half, :, 2 * DK:COLS].astype(F32)
        theirs = dkv_recv[0, half].astype(F32) + dkv_recv[2, half].astype(F32)
        for h in range(2):
            val_k = jnp.where(core == h, mine_k, theirs[:, 0:2 * DK]).astype(BF16)
            val_v = jnp.where(core == h, mine_v, theirs[:, 2 * DK:COLS]).astype(BF16)
            dk1_out[rows, h * DK:(h + 1) * DK] = val_k[:, 0:DK]
            dk2_out[rows, h * DK:(h + 1) * DK] = val_k[:, DK:2 * DK]
            dv_out[rows, h * DV:(h + 1) * DV] = val_v

    for cp in h_copies:
        cp.wait()
    total_tile = lam_send[2] + jnp.sum(lam_h[...], axis=0)
    total = -jnp.sum(jnp.sum(total_tile, axis=0, keepdims=True), axis=1, keepdims=True)
    lam_out[0:1, :] = total * e1 * lk1_ref[...]
    lam_out[1:2, :] = total * e1 * lq1_ref[...]
    lam_out[2:3, :] = -total * e2 * lk2_ref[...]
    lam_out[3:4, :] = -total * e2 * lq2_ref[...]

    for cp in first_copies():
        cp.wait_send()
    for j in range(1, LAST):
        for i in range(2):
            @pl.when(low_here(j) & (z > 0))
            def _():
                for cp in hop_copies(j, 0, i):
                    cp.wait_send()

            for cp in hop_copies(j, 1, i):
                cp.wait_send()
            for d in range(2):
                dq_copy(j, d, i).wait_send()


def finish(*refs):
    n = len(refs) // 2
    copies = [pltpu.make_async_copy(refs[i], refs[n + i], refs[-1].at[i]) for i in range(n)]
    for cp in copies:
        cp.start()
    for cp in copies:
        cp.wait()


def fused(*args):
    (q1, q2, k1, k2, v, go, lse1, lse2, d1, d2, starts, skip, lq1, lk1, lq2, lk2) = args
    rows = q1.shape[0]
    vm = pl.BlockSpec(memory_space=pltpu.VMEM)
    hbm = pl.BlockSpec(memory_space=pltpu.HBM)
    dma = pltpu.SemaphoreType.DMA
    lam_tile = (8, 2 * HALF)
    scratch = [
        pltpu.VMEM((2, 2 * HALF, COLS), BF16),
        pltpu.VMEM((2, 8, 2 * HALF), F32),
        pltpu.VMEM((2, 2 * HALF, COLS), BF16),
        pltpu.VMEM((2, PLANE, HALF, COLS), BF16),
        pltpu.VMEM((PLANES, 2, 2 * HALF, COLS), BF16),
        pltpu.VMEM((PLANES, 2, 2, 8, 2 * HALF), F32),
        pltpu.VMEM((2, 2 * HALF, 2 * DK), F32),
        pltpu.VMEM((PLANES, 2, 2 * HALF, 2 * DK), BF16),
        pltpu.VMEM((PLANES, 2, 2 * HALF, 2 * DK), BF16),
        pltpu.VMEM((2, HALF, 2 * DK), F32),
        pltpu.VMEM((2, HALF, 2 * DK), F32),
        pltpu.VMEM((2, HALF, 2 * DK), F32),
        pltpu.VMEM((2, 2, HALF, 2 * DK), BF16),
        pltpu.VMEM((2, PLANE * HALF, COLS), F32),
        pltpu.VMEM((3, 2, HALF, COLS), BF16),
        pltpu.VMEM((3, 2, HALF, COLS), BF16),
        pltpu.VMEM(lam_tile, F32),
        pltpu.VMEM((3,) + lam_tile, F32),
        pltpu.VMEM((LAST,) + lam_tile, F32),
        pltpu.VMEM((3,) + lam_tile, F32),
        pltpu.VMEM((HEAD_DEVICES - 1,) + lam_tile, F32),
        dma((2, 2, 3)),
        dma((PLANES, 2, 2)), dma((PLANES, 2, 2)),
        dma((PLANES, 2, 2)), dma((PLANES, 2)),
        dma((4,)), dma((2,)),
        dma((3, 2)), dma((3, 2)),
        dma((PLANES, 2, 2)), dma((PLANES, 2, 2)),
        dma((2, 2)), dma((2, 2)),
        dma, dma,
        dma((3, 2)), dma((3, 2)),
        dma((LAST,)), dma((LAST,)),
        dma((3,)), dma((3,)),
        dma((HEAD_DEVICES - 1,)), dma((HEAD_DEVICES - 1,)),
    ]
    outs = [jax.ShapeDtypeStruct(a.shape, BF16) for a in (q1, q2, k1, k2, v)]
    outs.append(jax.ShapeDtypeStruct((4, DK), F32))
    row = lambda a: a.reshape(1, DK)
    results = pl.pallas_call(
        kernel,
        out_shape=[pltpu.VMEM(o.shape, o.dtype) for o in outs],
        in_specs=[hbm] * 6 + [vm] * 5 + [pl.BlockSpec(memory_space=pltpu.SMEM)] + [vm] * 4,
        out_specs=[vm] * 6,
        scratch_shapes=scratch,
        compiler_params=pltpu.CompilerParams(
            collective_id=0, has_side_effects=True, vmem_limit_bytes=VMEM_LIMIT
        ),
    )(
        q1, q2, go, k1, k2, v, lse1, lse2, d1, d2, starts.reshape(DEVICES, rows), skip,
        row(lq1), row(lk1), row(lq2), row(lk2),
    )
    return pl.pallas_call(
        finish,
        out_shape=outs,
        in_specs=[vm] * 6,
        out_specs=[hbm] * 6,
        scratch_shapes=[dma((6,))],
        compiler_params=pltpu.CompilerParams(vmem_limit_bytes=8 * 1024 * 1024),
    )(*results)


def solution(mesh):
    tok = P("seq", "head")
    stat = P("head", "seq")
    return jax.shard_map(
        fused,
        mesh=mesh,
        in_specs=(tok,) * 6 + (stat,) * 4 + (P(),) * 6,
        out_specs=(tok,) * 5 + (P(),),
        check_vma=False,
    )
```

```python
import math

import jax
import jax.numpy as jnp
from jax import lax
from jax.experimental import pallas as pl
from jax.experimental.pallas import tpu as pltpu
from jax.sharding import PartitionSpec as P

MESH = pl.DeviceIdType.MESH
LAMBDA_INIT = 0.8 - 0.6 * math.exp(-3.6)
F32 = jnp.float32
BF16 = jnp.bfloat16

DK = 128
DV = 256
HALF = 64
COLS = 2 * DK + DV
PLANE = 4
PLANES = 8
DEVICES = PLANE * PLANES
HEAD_DEVICES = 8
LAST = PLANES - 1
FAR = 8192
VMEM_LIMIT = 60 * 1024 * 1024


def nt_dot(a, b):
    return lax.dot_general(a, b, (((1,), (1,)), ((), ())), preferred_element_type=F32)


def tn_dot(a, b):
    return lax.dot_general(a, b, (((0,), (0,)), ((), ())), preferred_element_type=F32)


def nn_dot(a, b):
    return lax.dot_general(a, b, (((1,), (0,)), ((), ())), preferred_element_type=F32)


def kernel(
    q1_ref, q2_ref, go_ref, k1_ref, k2_ref, v_ref,
    lse1_hbm, lse2_hbm, del1_hbm, del2_hbm, starts_hbm, skip_hbm,
    lq1_hbm, lk1_hbm, lq2_hbm, lk2_hbm,
    dq1_out, dq2_out, dk1_out, dk2_out, dv_out, lam_out,
    lse1_ref, lse2_ref, del1_ref, del2_ref, starts_ref, skip_ref,
    lq1_ref, lk1_ref, lq2_ref, lk2_ref,
    qpay, spay, kpay, kbuf, qbuf, sbuf,
    dqp, dqs, dqr, loc_send, loc_recv, fin,
    dkv, dkv_send, dkv_recv,
    lam_acc, lam_send, lam_x, lam_z, lam_y,
    in_sem, small_sem, q_send, q_recv, s_send, s_recv, q0_sem, s0_sem, k_send, k_recv,
    d_send, d_recv, f_send, f_recv, l_send, l_recv, o_send, o_recv,
    x_send, x_recv, z_send, z_recv, y_send, y_recv,
):
    me = lax.axis_index("seq")
    hme = lax.axis_index("head")
    z = me // PLANE
    t_me = lax.rem(me, PLANE)
    col = t_me // 2
    core = lax.rem(t_me, 2)
    other = 1 - core
    zdn = lax.rem(z + PLANES - 1, PLANES)
    zup = lax.rem(z + 1, PLANES)

    def dev(zz, cc, kk):
        return zz * PLANE + cc * 2 + kk

    peers = [dev(z, col, other), dev(z, 1 - col, core), dev(z, 1 - col, other)]
    peer_head = [other, core, other]
    peer_t = [2 * col + other, 2 * (1 - col) + core, 2 * (1 - col) + other]
    ring = [zdn, zup]

    def send(src, dst, s_sem, r_sem, seq):
        return pltpu.make_async_remote_copy(
            src_ref=src, dst_ref=dst, send_sem=s_sem, recv_sem=r_sem,
            device_id={"seq": seq}, device_id_type=MESH,
        )

    across = lax.rem(hme + HEAD_DEVICES // 2, HEAD_DEVICES)
    y_me = lax.rem(hme, HEAD_DEVICES // 2)
    beside = [hme - y_me + lax.rem(y_me + off, HEAD_DEVICES // 2) for off in range(1, HEAD_DEVICES // 2)]

    barrier = pltpu.get_barrier_semaphore()
    for p in peers:
        pl.semaphore_signal(barrier, inc=1, device_id={"seq": p}, device_id_type=MESH)
    for off in range(1, PLANES):
        zz = lax.rem(z + off, PLANES)
        pl.semaphore_signal(barrier, inc=1, device_id={"seq": dev(zz, col, core)}, device_id_type=MESH)
    for zz in (zdn, zup):
        pl.semaphore_signal(barrier, inc=1, device_id={"seq": dev(zz, col, other)}, device_id_type=MESH)
    for t in range(PLANE):
        pl.semaphore_signal(
            barrier, inc=1, device_id={"seq": z * PLANE + t, "head": across}, device_id_type=MESH
        )
    for yy in beside:
        pl.semaphore_signal(barrier, inc=1, device_id={"head": yy}, device_id_type=MESH)

    packs = []
    for n, (pay, parts) in enumerate(((kpay, (k1_ref, k2_ref, v_ref)), (qpay, (q1_ref, q2_ref, go_ref)))):
        for h in range(2):
            for i, (ref, at, width) in enumerate(zip(parts, (0, DK, 2 * DK), (DK, DK, DV))):
                cp = pltpu.make_async_copy(
                    ref.at[:, h * width:(h + 1) * width], pay.at[h, :, at:at + width], in_sem.at[n, h, i]
                )
                cp.start()
                packs.append(cp)
    small = [
        pltpu.make_async_copy(a, b, small_sem.at[i])
        for i, (a, b) in enumerate((
            (lse1_hbm, lse1_ref), (lse2_hbm, lse2_ref), (del1_hbm, del1_ref), (del2_hbm, del2_ref),
            (starts_hbm, starts_ref), (skip_hbm, skip_ref),
            (lq1_hbm, lq1_ref), (lk1_hbm, lk1_ref), (lq2_hbm, lq2_ref), (lk2_hbm, lk2_ref),
        ))
    ]
    for cp in small:
        cp.start()

    for cp in small:
        cp.wait()
    for h in range(2):
        for i, ref in enumerate((lse1_ref, lse2_ref, del1_ref, del2_ref)):
            spay[h, i:i + 1, :] = ref[h:h + 1, :]
        spay[h, 4:8, :] = jnp.zeros((4, 128), F32)
    dkv[...] = jnp.zeros_like(dkv)
    lam_acc[...] = jnp.zeros_like(lam_acc)

    my_rows = pl.ds(pl.multiple_of(core * HALF, HALF), HALF)
    for cp in packs:
        cp.wait()

    pl.semaphore_wait(barrier, 3 + LAST + 2 + PLANE + 3)

    def first_copies():
        out = []
        for d in range(2):
            for i, (h, k) in enumerate(((core, core), (other, other))):
                to = dev(ring[d], col, k)
                out.append(send(
                    qpay.at[h, d * HALF:(d + 1) * HALF], qbuf.at[1, d, my_rows, :], q_send.at[0, d, i],
                    q_recv.at[1, d, core], to))
                out.append(send(spay.at[h], sbuf.at[1, d, core], s_send.at[0, d, i], s_recv.at[1, d], to))
        return out

    def key_copies():
        return [
            send(kpay.at[peer_head[i], half * HALF:(half + 1) * HALF], kbuf.at[half, t_me], k_send.at[i, half],
                 k_recv.at[i, half], peers[i])
            for half in range(2) for i in range(3)
        ]

    def pair_copies():
        return [
            send(qpay.at[other, 0:HALF], qbuf.at[0, 0, my_rows, :], q0_sem.at[0], q0_sem.at[1], peers[0]),
            send(qpay.at[other, HALF:2 * HALF], qbuf.at[0, 1, my_rows, :], q0_sem.at[2], q0_sem.at[3], peers[0]),
            send(spay.at[other], sbuf.at[0, 0, core], s0_sem.at[0], s0_sem.at[1], peers[0]),
        ]

    @pl.when(core == 0)
    def _():
        for cp in first_copies():
            cp.start()

    for cp in pair_copies():
        cp.start()
    for cp in key_copies():
        cp.start()
    for cp in pair_copies():
        cp.wait()

    @pl.when(core == 1)
    def _():
        for cp in first_copies():
            cp.start()

    sbuf[0, 0, core] = spay[core]
    for half in range(2):
        qbuf[0, half, my_rows, :] = qpay[core, half * HALF:(half + 1) * HALF]
        kbuf[half, t_me] = kpay[core, half * HALF:(half + 1) * HALF]

    e1 = jnp.exp(jnp.sum(lq1_ref[...] * lk1_ref[...], axis=1, keepdims=True))
    e2 = jnp.exp(jnp.sum(lq2_ref[...] * lk2_ref[...], axis=1, keepdims=True))
    mixing = e1 - e2 + LAMBDA_INIT
    scale = DK ** -0.5

    def piece(i):
        return slice(i * HALF, (i + 1) * HALF)

    def hop_copies(j, d, i):
        to = dev(ring[d], col, core)
        out = [send(qbuf.at[j, d, piece(i)], qbuf.at[j + 1, d, piece(i)], q_send.at[j, d, i], q_recv.at[j + 1, d, i], to)]
        if i == 1:
            out.append(send(sbuf.at[j, d], sbuf.at[j + 1, d], s_send.at[j, d, 0], s_recv.at[j + 1, d], to))
        return out

    def dq_copy(j, d, i):
        return send(dqs.at[j, d, piece(i)], dqr.at[j + 1, d, piece(i)], d_send.at[j, d, i], d_recv.at[j + 1, d, i],
                    dev(ring[d], col, core))

    def low_here(j):
        return z + j <= LAST

    def wait_piece(j, d, i):
        block = qbuf.at[j, d, piece(i)]
        pltpu.make_async_copy(block, block, q_recv.at[j, d, i]).wait()
        if i == 1:
            pltpu.make_async_copy(sbuf.at[j, d], sbuf.at[j, d], s_recv.at[j, d]).wait()

    lane = lax.broadcasted_iota(jnp.int32, (1, 2 * HALF), 1)
    first = lane < HALF
    sub = lax.broadcasted_iota(jnp.int32, (HALF, 1), 0)

    def merge(a, b, d):
        if d == 0:
            return jnp.where(first, a, pltpu.roll(b, HALF, 1))
        return jnp.where(first, pltpu.roll(a, HALF, 1), b)

    def tile(j, sd, d, zq, kh):
        stats = merge(sbuf[j, sd, 0], sbuf[j, sd, 1], d)
        lse_a, lse_b, del_a, del_b = (stats[i:i + 1] for i in range(4))
        host = PLANE * zq + 2 * col
        starts = merge(starts_ref[pl.ds(host, 1), :], starts_ref[pl.ds(host + 1, 1), :], d)
        if d == 0:
            qpos = host * HALF + lane
        else:
            qpos = jnp.where(first, (2 * DEVICES - 1 - host) * HALF + lane, (2 * DEVICES - 3 - host) * HALF + lane)
        seen = []
        for t in range(PLANE):
            khost = PLANE * z + t
            base = khost * HALF if kh == 0 else (2 * DEVICES - 1 - khost) * HALF
            skip_a = skip_ref[lax.rem(khost - host + DEVICES, DEVICES), khost]
            skip_b = skip_ref[lax.rem(khost - host - 1 + DEVICES, DEVICES), khost]
            start = starts - base + jnp.where(first, skip_a, skip_b) * FAR
            seen.append((sub >= start) & (sub <= qpos - base))
        visible = jnp.concatenate(seen, axis=0)
        qa = qbuf[j, d, :, 0:DK]
        qb = qbuf[j, d, :, DK:2 * DK]
        g = qbuf[j, d, :, 2 * DK:COLS]
        keys = kbuf[kh].reshape(PLANE * HALF, COLS)
        ka, kb, vals = keys[:, 0:DK], keys[:, DK:2 * DK], keys[:, 2 * DK:COLS]
        pa = jnp.where(visible, jnp.exp(nt_dot(ka, qa) * scale - lse_a), 0.0)
        pb = jnp.where(visible, jnp.exp(nt_dot(kb, qb) * scale - lse_b), 0.0)
        inner = nt_dot(vals, g)
        dsa = (pa * (inner - del_a)).astype(BF16)
        dsb = (pb * (-mixing * inner - del_b)).astype(BF16)
        mix = (pa - mixing * pb).astype(BF16)
        lam_acc[...] += jnp.sum((pb * inner).reshape(PLANE * HALF // 8, 8, 2 * HALF), axis=0)
        dkv[kh, :, 0:DK] += nn_dot(dsa, qa)
        dkv[kh, :, DK:2 * DK] += nn_dot(dsb, qb)
        dkv[kh, :, 2 * DK:COLS] += nn_dot(mix, g)
        dqp[j, d, :, 0:DK] += tn_dot(dsa, ka) * scale
        dqp[j, d, :, DK:2 * DK] += tn_dot(dsb, kb) * scale

    def home_copies(half):
        return [
            send(
                dkv_send.at[i, half], dkv_recv.at[i, half], o_send.at[i, half], o_recv.at[i, half], peers[i],
            )
            for i in range(3)
        ]

    def send_home(half):
        for i in range(3):
            rows = pl.ds(pl.multiple_of(peer_t[i] * HALF, HALF), HALF)
            dkv_send[i, half, :, 0:2 * DK] = (dkv[half, rows, 0:2 * DK] * scale).astype(BF16)
            dkv_send[i, half, :, 2 * DK:COLS] = dkv[half, rows, 2 * DK:COLS].astype(BF16)
        for cp in home_copies(half):
            cp.start()

    def work(j, d):
        dqp[j, d] = jnp.zeros((2 * HALF, 2 * DK), F32)
        if d == 0:
            @pl.when(low_here(j))
            def _():
                tile(j, 0, 0, z + j, 0)
        else:
            zq = lax.rem(z - j + PLANES, PLANES)
            tile(j, 1, 1, zq, 0)

            @pl.when(j <= z)
            def _():
                tile(j, 1, 1, zq, 1)

    def relay(j, i, last):
        @pl.when(low_here(j))
        def _():
            wait_piece(j, 0, i)

        if last is not True:
            @pl.when(low_here(j) & (z > 0) & jnp.logical_not(last))
            def _():
                for cp in hop_copies(j, 0, i):
                    cp.start()

        wait_piece(j, 1, i)
        if last is not True:
            @pl.when(jnp.logical_not(last))
            def _():
                for cp in hop_copies(j, 1, i):
                    cp.start()

    def pass_sums(j, d, first_hop):
        for i in range(2):
            part = dqp[j, d, piece(i)]
            if not first_hop:
                block = dqr.at[j, d, piece(i)]
                pltpu.make_async_copy(block, block, d_recv.at[j, d, i]).wait()
                part = part + dqr[j, d, piece(i)].astype(F32)
            dqs[j, d, piece(i)] = part.astype(BF16)
            if j is not LAST:
                dq_copy(j, d, i).start()

    for i in range(2):
        for d in range(2):
            wait_piece(1, d, i)

            @pl.when((d == 1) | (low_here(1) & (z > 0)))
            def _():
                for cp in hop_copies(1, d, i):
                    cp.start()
    for i in range(2):
        relay(2, i, False)

    for cp in key_copies():
        cp.wait()
    for d in range(2):
        dqp[0, d] = jnp.zeros((2 * HALF, 2 * DK), F32)
    tile(0, 0, 0, z, 0)
    tile(0, 0, 1, z, 0)
    tile(0, 0, 1, z, 1)
    their_rows = pl.ds(pl.multiple_of(other * HALF, HALF), HALF)
    for d in range(2):
        loc_send[d] = dqp[0, d, their_rows, :]
    loc_copy = send(loc_send, loc_recv, l_send, l_recv, peers[0])
    loc_copy.start()

    @pl.when(z == 0)
    def _():
        send_home(1)

    def step(j, carry):
        @pl.when(j > 2)
        def _():
            relay(j, 0, j == LAST)
            relay(j, 1, j == LAST)

        for d in range(2):
            @pl.when(j == 2)
            def _():
                pass_sums(1, d, True)

            @pl.when(j > 2)
            def _():
                pass_sums(j - 1, d, False)

        for d in range(2):
            work(j, d)

        @pl.when(j == z)
        def _():
            send_home(1)

        return carry

    lax.fori_loop(1, LAST + 1, step, 0)

    def fin_copies(d):
        out = []
        for i, k in enumerate((core, other)):
            rows = pl.ds(pl.multiple_of(k * HALF, HALF), HALF)
            out.append(
                send(dqs.at[LAST, d, rows, :], fin.at[d, core], f_send.at[d, i], f_recv.at[d, i], dev(ring[d], col, k))
            )
        return out

    x_copies = [send(lam_send.at[0], lam_x.at[i], x_send.at[i], x_recv.at[i], peers[i]) for i in range(3)] + [
        pltpu.make_async_remote_copy(
            src_ref=lam_send.at[0], dst_ref=lam_x.at[3 + i], send_sem=x_send.at[3 + i], recv_sem=x_recv.at[3 + i],
            device_id={"seq": to, "head": across}, device_id_type=MESH,
        )
        for i, to in enumerate([me] + peers)
    ]
    z_copies = [
        send(lam_send.at[1], lam_z.at[off - 1], z_send.at[off - 1], z_recv.at[off - 1],
             dev(lax.rem(z + off, PLANES), col, core))
        for off in range(1, PLANES)
    ]
    y_copies = [
        pltpu.make_async_remote_copy(
            src_ref=lam_send.at[2], dst_ref=lam_y.at[i], send_sem=y_send.at[i], recv_sem=y_recv.at[i],
            device_id={"head": to}, device_id_type=MESH,
        )
        for i, to in enumerate(beside)
    ]

    def lam_stage(n):
        if n > 0:
            parts = (x_copies, z_copies)[n - 1]
            for cp in parts:
                cp.wait()
            lam_send[n] = lam_send[n - 1] + jnp.sum((lam_x, lam_z)[n - 1][...], axis=0)
        else:
            lam_send[0] = lam_acc[...]
        for cp in (x_copies, z_copies, y_copies)[n]:
            cp.start()

    lam_stage(0)
    send_home(0)
    lam_stage(1)
    for d in range(2):
        pass_sums(LAST, d, False)
        for cp in fin_copies(d):
            cp.start()
    lam_stage(2)

    key_rows = pl.ds(pl.multiple_of(t_me * HALF, HALF), HALF)
    for half in (1, 0):
        for cp in home_copies(half):
            cp.wait()
        rows = slice(half * HALF, (half + 1) * HALF)
        own = dkv[half, key_rows, :]
        mine_k = own[:, 0:2 * DK] * scale + dkv_recv[1, half, :, 0:2 * DK].astype(F32)
        mine_v = own[:, 2 * DK:COLS] + dkv_recv[1, half, :, 2 * DK:COLS].astype(F32)
        theirs = dkv_recv[0, half].astype(F32) + dkv_recv[2, half].astype(F32)
        for h in range(2):
            val_k = jnp.where(core == h, mine_k, theirs[:, 0:2 * DK]).astype(BF16)
            val_v = jnp.where(core == h, mine_v, theirs[:, 2 * DK:COLS]).astype(BF16)
            dk1_out[rows, h * DK:(h + 1) * DK] = val_k[:, 0:DK]
            dk2_out[rows, h * DK:(h + 1) * DK] = val_k[:, DK:2 * DK]
            dv_out[rows, h * DV:(h + 1) * DV] = val_v

    loc_copy.wait()
    for d in range(2):
        for cp in fin_copies(d):
            cp.wait()
        rows = slice(d * HALF, (d + 1) * HALF)
        mine = dqp[0, d, my_rows, :] + fin[d, core].astype(F32)
        theirs = loc_recv[d] + fin[d, other].astype(F32)
        for h in range(2):
            val = jnp.where(core == h, mine, theirs).astype(BF16)
            dq1_out[rows, h * DK:(h + 1) * DK] = val[:, 0:DK]
            dq2_out[rows, h * DK:(h + 1) * DK] = val[:, DK:2 * DK]

    for cp in y_copies:
        cp.wait()
    total_tile = lam_send[2] + jnp.sum(lam_y[...], axis=0)
    total = -jnp.sum(jnp.sum(total_tile, axis=0, keepdims=True), axis=1, keepdims=True)
    lam_out[0:1, :] = total * e1 * lk1_ref[...]
    lam_out[1:2, :] = total * e1 * lq1_ref[...]
    lam_out[2:3, :] = -total * e2 * lk2_ref[...]
    lam_out[3:4, :] = -total * e2 * lq2_ref[...]

    for cp in first_copies():
        cp.wait_send()
    for j in range(1, LAST):
        for i in range(2):
            @pl.when(low_here(j) & (z > 0))
            def _():
                for cp in hop_copies(j, 0, i):
                    cp.wait_send()

            for cp in hop_copies(j, 1, i):
                cp.wait_send()
            for d in range(2):
                dq_copy(j, d, i).wait_send()


def finish(*refs):
    n = len(refs) // 2
    copies = [pltpu.make_async_copy(refs[i], refs[n + i], refs[-1].at[i]) for i in range(n)]
    for cp in copies:
        cp.start()
    for cp in copies:
        cp.wait()


def fused(*args):
    (q1, q2, k1, k2, v, go, lse1, lse2, d1, d2, starts, skip, lq1, lk1, lq2, lk2) = args
    rows = q1.shape[0]
    vm = pl.BlockSpec(memory_space=pltpu.VMEM)
    hbm = pl.BlockSpec(memory_space=pltpu.HBM)
    dma = pltpu.SemaphoreType.DMA
    lam_tile = (8, 2 * HALF)
    scratch = [
        *[pltpu.VMEM((2, 2 * HALF), F32)] * 4,
        pltpu.VMEM((DEVICES, 2 * HALF), jnp.int32),
        pltpu.SMEM((DEVICES, DEVICES), jnp.int32),
        *[pltpu.VMEM((1, DK), F32)] * 4,
        pltpu.VMEM((2, 2 * HALF, COLS), BF16),
        pltpu.VMEM((2, 8, 2 * HALF), F32),
        pltpu.VMEM((2, 2 * HALF, COLS), BF16),
        pltpu.VMEM((2, PLANE, HALF, COLS), BF16),
        pltpu.VMEM((PLANES, 2, 2 * HALF, COLS), BF16),
        pltpu.VMEM((PLANES, 2, 2, 8, 2 * HALF), F32),
        pltpu.VMEM((PLANES, 2, 2 * HALF, 2 * DK), F32),
        pltpu.VMEM((PLANES, 2, 2 * HALF, 2 * DK), BF16),
        pltpu.VMEM((PLANES, 2, 2 * HALF, 2 * DK), BF16),
        pltpu.VMEM((2, HALF, 2 * DK), F32),
        pltpu.VMEM((2, HALF, 2 * DK), F32),
        pltpu.VMEM((2, 2, HALF, 2 * DK), BF16),
        pltpu.VMEM((2, PLANE * HALF, COLS), F32),
        pltpu.VMEM((3, 2, HALF, COLS), BF16),
        pltpu.VMEM((3, 2, HALF, COLS), BF16),
        pltpu.VMEM(lam_tile, F32),
        pltpu.VMEM((3,) + lam_tile, F32),
        pltpu.VMEM((LAST,) + lam_tile, F32),
        pltpu.VMEM((LAST,) + lam_tile, F32),
        pltpu.VMEM((3,) + lam_tile, F32),
        dma((2, 2, 3)), dma((10,)),
        dma((PLANES, 2, 2)), dma((PLANES, 2, 2)),
        dma((PLANES, 2, 2)), dma((PLANES, 2)),
        dma((4,)), dma((2,)),
        dma((3, 2)), dma((3, 2)),
        dma((PLANES, 2, 2)), dma((PLANES, 2, 2)),
        dma((2, 2)), dma((2, 2)),
        dma, dma,
        dma((3, 2)), dma((3, 2)),
        dma((LAST,)), dma((LAST,)),
        dma((LAST,)), dma((LAST,)),
        dma((3,)), dma((3,)),
    ]
    outs = [jax.ShapeDtypeStruct(a.shape, BF16) for a in (q1, q2, k1, k2, v)]
    outs.append(jax.ShapeDtypeStruct((4, DK), F32))
    row = lambda a: a.reshape(1, DK)
    results = pl.pallas_call(
        kernel,
        out_shape=[pltpu.VMEM(o.shape, o.dtype) for o in outs],
        in_specs=[hbm] * 16,
        out_specs=[vm] * 6,
        scratch_shapes=scratch,
        compiler_params=pltpu.CompilerParams(
            collective_id=0, has_side_effects=True, vmem_limit_bytes=VMEM_LIMIT
        ),
    )(
        q1, q2, go, k1, k2, v, lse1, lse2, d1, d2, starts.reshape(DEVICES, rows), skip,
        row(lq1), row(lk1), row(lq2), row(lk2),
    )
    return pl.pallas_call(
        finish,
        out_shape=outs,
        in_specs=[vm] * 6,
        out_specs=[hbm] * 6,
        scratch_shapes=[dma((6,))],
        compiler_params=pltpu.CompilerParams(vmem_limit_bytes=8 * 1024 * 1024),
    )(*results)


def solution(mesh):
    tok = P("seq", "head")
    stat = P("head", "seq")
    return jax.shard_map(
        fused,
        mesh=mesh,
        in_specs=(tok,) * 6 + (stat,) * 4 + (P(),) * 6,
        out_specs=(tok,) * 5 + (P(),),
        check_vma=False,
    )
```

```python
import math

import jax
import jax.numpy as jnp
from jax import lax
from jax.experimental import pallas as pl
from jax.experimental.pallas import tpu as pltpu
from jax.sharding import PartitionSpec as P

MESH = pl.DeviceIdType.MESH
LAMBDA_INIT = 0.8 - 0.6 * math.exp(-3.6)
F32 = jnp.float32
BF16 = jnp.bfloat16

DK = 128
DV = 256
HALF = 64
COLS = 2 * DK + DV
PLANE = 4
PLANES = 8
DEVICES = PLANE * PLANES
HEAD_DEVICES = 8
LAST = PLANES - 1
FAR = 8192
VMEM_LIMIT = 60 * 1024 * 1024


def nt_dot(a, b):
    return lax.dot_general(a, b, (((1,), (1,)), ((), ())), preferred_element_type=F32)


def tn_dot(a, b):
    return lax.dot_general(a, b, (((0,), (0,)), ((), ())), preferred_element_type=F32)


def nn_dot(a, b):
    return lax.dot_general(a, b, (((1,), (0,)), ((), ())), preferred_element_type=F32)


def kernel(
    q1_ref, q2_ref, go_ref, k1_ref, k2_ref, v_ref,
    lse1_hbm, lse2_hbm, del1_hbm, del2_hbm, starts_hbm, skip_hbm,
    lq1_hbm, lk1_hbm, lq2_hbm, lk2_hbm,
    dq1_out, dq2_out, dk1_out, dk2_out, dv_out, lam_out,
    lse1_ref, lse2_ref, del1_ref, del2_ref, starts_ref, skip_ref,
    lq1_ref, lk1_ref, lq2_ref, lk2_ref,
    qpay, spay, kpay, kbuf, qbuf, sbuf,
    dqp, dqs, dqr, loc_send, loc_recv, fin,
    dkv, dkv_send, dkv_recv,
    lam_acc, lam_send, lam_x, lam_z, lam_y,
    in_sem, small_sem, q_send, q_recv, s_send, s_recv, q0_sem, s0_sem, k_send, k_recv,
    d_send, d_recv, f_send, f_recv, l_send, l_recv, o_send, o_recv,
    x_send, x_recv, z_send, z_recv, y_send, y_recv,
):
    me = lax.axis_index("seq")
    hme = lax.axis_index("head")
    z = me // PLANE
    t_me = lax.rem(me, PLANE)
    col = t_me // 2
    core = lax.rem(t_me, 2)
    other = 1 - core
    zdn = lax.rem(z + PLANES - 1, PLANES)
    zup = lax.rem(z + 1, PLANES)

    def dev(zz, cc, kk):
        return zz * PLANE + cc * 2 + kk

    peers = [dev(z, col, other), dev(z, 1 - col, core), dev(z, 1 - col, other)]
    peer_head = [other, core, other]
    peer_t = [2 * col + other, 2 * (1 - col) + core, 2 * (1 - col) + other]
    ring = [zdn, zup]

    def send(src, dst, s_sem, r_sem, seq):
        return pltpu.make_async_remote_copy(
            src_ref=src, dst_ref=dst, send_sem=s_sem, recv_sem=r_sem,
            device_id={"seq": seq}, device_id_type=MESH,
        )

    across = lax.rem(hme + HEAD_DEVICES // 2, HEAD_DEVICES)
    y_me = lax.rem(hme, HEAD_DEVICES // 2)
    beside = [hme - y_me + lax.rem(y_me + off, HEAD_DEVICES // 2) for off in range(1, HEAD_DEVICES // 2)]

    barrier = pltpu.get_barrier_semaphore()
    for p in peers:
        pl.semaphore_signal(barrier, inc=1, device_id={"seq": p}, device_id_type=MESH)
    for off in range(1, PLANES):
        zz = lax.rem(z + off, PLANES)
        pl.semaphore_signal(barrier, inc=1, device_id={"seq": dev(zz, col, core)}, device_id_type=MESH)
    for zz in (zdn, zup):
        pl.semaphore_signal(barrier, inc=1, device_id={"seq": dev(zz, col, other)}, device_id_type=MESH)
    for t in range(PLANE):
        pl.semaphore_signal(
            barrier, inc=1, device_id={"seq": z * PLANE + t, "head": across}, device_id_type=MESH
        )
    for yy in beside:
        pl.semaphore_signal(barrier, inc=1, device_id={"head": yy}, device_id_type=MESH)

    packs = []
    for n, (pay, parts) in enumerate(((kpay, (k1_ref, k2_ref, v_ref)), (qpay, (q1_ref, q2_ref, go_ref)))):
        for h in range(2):
            for i, (ref, at, width) in enumerate(zip(parts, (0, DK, 2 * DK), (DK, DK, DV))):
                cp = pltpu.make_async_copy(
                    ref.at[:, h * width:(h + 1) * width], pay.at[h, :, at:at + width], in_sem.at[n, h, i]
                )
                cp.start()
                packs.append(cp)
    small = [
        pltpu.make_async_copy(a, b, small_sem.at[i])
        for i, (a, b) in enumerate((
            (lse1_hbm, lse1_ref), (lse2_hbm, lse2_ref), (del1_hbm, del1_ref), (del2_hbm, del2_ref),
            (starts_hbm, starts_ref), (skip_hbm, skip_ref),
            (lq1_hbm, lq1_ref), (lk1_hbm, lk1_ref), (lq2_hbm, lq2_ref), (lk2_hbm, lk2_ref),
        ))
    ]
    for cp in small:
        cp.start()

    for cp in small:
        cp.wait()
    for h in range(2):
        for i, ref in enumerate((lse1_ref, lse2_ref, del1_ref, del2_ref)):
            spay[h, i:i + 1, :] = ref[h:h + 1, :]
        spay[h, 4:8, :] = jnp.zeros((4, 128), F32)
    dkv[...] = jnp.zeros_like(dkv)
    lam_acc[...] = jnp.zeros_like(lam_acc)

    my_rows = pl.ds(pl.multiple_of(core * HALF, HALF), HALF)
    for cp in packs:
        cp.wait()

    pl.semaphore_wait(barrier, 3 + LAST + 2 + PLANE + 3)

    def first_copies():
        out = []
        for d in range(2):
            for i, (h, k) in enumerate(((core, core), (other, other))):
                to = dev(ring[d], col, k)
                out.append(send(
                    qpay.at[h, d * HALF:(d + 1) * HALF], qbuf.at[1, d, my_rows, :], q_send.at[0, d, i],
                    q_recv.at[1, d, core], to))
                out.append(send(spay.at[h], sbuf.at[1, d, core], s_send.at[0, d, i], s_recv.at[1, d], to))
        return out

    def key_copies():
        return [
            send(kpay.at[peer_head[i], half * HALF:(half + 1) * HALF], kbuf.at[half, t_me], k_send.at[i, half],
                 k_recv.at[i, half], peers[i])
            for half in range(2) for i in range(3)
        ]

    def pair_copies():
        return [
            send(qpay.at[other, 0:HALF], qbuf.at[0, 0, my_rows, :], q0_sem.at[0], q0_sem.at[1], peers[0]),
            send(qpay.at[other, HALF:2 * HALF], qbuf.at[0, 1, my_rows, :], q0_sem.at[2], q0_sem.at[3], peers[0]),
            send(spay.at[other], sbuf.at[0, 0, core], s0_sem.at[0], s0_sem.at[1], peers[0]),
        ]

    @pl.when(core == 0)
    def _():
        for cp in first_copies():
            cp.start()

    for cp in pair_copies():
        cp.start()
    for cp in key_copies():
        cp.start()
    for cp in pair_copies():
        cp.wait()

    @pl.when(core == 1)
    def _():
        for cp in first_copies():
            cp.start()

    sbuf[0, 0, core] = spay[core]
    for half in range(2):
        qbuf[0, half, my_rows, :] = qpay[core, half * HALF:(half + 1) * HALF]
        kbuf[half, t_me] = kpay[core, half * HALF:(half + 1) * HALF]

    e1 = jnp.exp(jnp.sum(lq1_ref[...] * lk1_ref[...], axis=1, keepdims=True))
    e2 = jnp.exp(jnp.sum(lq2_ref[...] * lk2_ref[...], axis=1, keepdims=True))
    mixing = e1 - e2 + LAMBDA_INIT
    scale = DK ** -0.5

    def piece(i):
        return slice(i * HALF, (i + 1) * HALF)

    def hop_copies(j, d, i):
        to = dev(ring[d], col, core)
        out = [send(qbuf.at[j, d, piece(i)], qbuf.at[j + 1, d, piece(i)], q_send.at[j, d, i], q_recv.at[j + 1, d, i], to)]
        if i == 1:
            out.append(send(sbuf.at[j, d], sbuf.at[j + 1, d], s_send.at[j, d, 0], s_recv.at[j + 1, d], to))
        return out

    def dq_copy(j, d, i):
        return send(dqs.at[j, d, piece(i)], dqr.at[j + 1, d, piece(i)], d_send.at[j, d, i], d_recv.at[j + 1, d, i],
                    dev(ring[d], col, core))

    def low_here(j):
        return z + j <= LAST

    def wait_piece(j, d, i):
        block = qbuf.at[j, d, piece(i)]
        pltpu.make_async_copy(block, block, q_recv.at[j, d, i]).wait()
        if i == 1:
            pltpu.make_async_copy(sbuf.at[j, d], sbuf.at[j, d], s_recv.at[j, d]).wait()

    lane = lax.broadcasted_iota(jnp.int32, (1, 2 * HALF), 1)
    first = lane < HALF
    sub = lax.broadcasted_iota(jnp.int32, (HALF, 1), 0)

    def merge(a, b, d):
        if d == 0:
            return jnp.where(first, a, pltpu.roll(b, HALF, 1))
        return jnp.where(first, pltpu.roll(a, HALF, 1), b)

    def tile(j, sd, d, zq, kh):
        stats = merge(sbuf[j, sd, 0], sbuf[j, sd, 1], d)
        lse_a, lse_b, del_a, del_b = (stats[i:i + 1] for i in range(4))
        host = PLANE * zq + 2 * col
        starts = merge(starts_ref[pl.ds(host, 1), :], starts_ref[pl.ds(host + 1, 1), :], d)
        if d == 0:
            qpos = host * HALF + lane
        else:
            qpos = jnp.where(first, (2 * DEVICES - 1 - host) * HALF + lane, (2 * DEVICES - 3 - host) * HALF + lane)
        seen = []
        for t in range(PLANE):
            khost = PLANE * z + t
            base = khost * HALF if kh == 0 else (2 * DEVICES - 1 - khost) * HALF
            skip_a = skip_ref[lax.rem(khost - host + DEVICES, DEVICES), khost]
            skip_b = skip_ref[lax.rem(khost - host - 1 + DEVICES, DEVICES), khost]
            start = starts - base + jnp.where(first, skip_a, skip_b) * FAR
            seen.append((sub >= start) & (sub <= qpos - base))
        visible = jnp.concatenate(seen, axis=0)
        qa = qbuf[j, d, :, 0:DK]
        qb = qbuf[j, d, :, DK:2 * DK]
        g = qbuf[j, d, :, 2 * DK:COLS]
        keys = kbuf[kh].reshape(PLANE * HALF, COLS)
        ka, kb, vals = keys[:, 0:DK], keys[:, DK:2 * DK], keys[:, 2 * DK:COLS]
        pa = jnp.where(visible, jnp.exp(nt_dot(ka, qa) * scale - lse_a), 0.0)
        pb = jnp.where(visible, jnp.exp(nt_dot(kb, qb) * scale - lse_b), 0.0)
        inner = nt_dot(vals, g)
        dsa = (pa * (inner - del_a)).astype(BF16)
        dsb = (pb * (-mixing * inner - del_b)).astype(BF16)
        mix = (pa - mixing * pb).astype(BF16)
        lam_acc[...] += jnp.sum((pb * inner).reshape(PLANE * HALF // 8, 8, 2 * HALF), axis=0)
        dkv[kh, :, 0:DK] += nn_dot(dsa, qa)
        dkv[kh, :, DK:2 * DK] += nn_dot(dsb, qb)
        dkv[kh, :, 2 * DK:COLS] += nn_dot(mix, g)
        dqp[j, d, :, 0:DK] += tn_dot(dsa, ka) * scale
        dqp[j, d, :, DK:2 * DK] += tn_dot(dsb, kb) * scale

    def home_copies(half):
        return [
            send(
                dkv_send.at[i, half], dkv_recv.at[i, half], o_send.at[i, half], o_recv.at[i, half], peers[i],
            )
            for i in range(3)
        ]

    def send_home(half):
        for i in range(3):
            rows = pl.ds(pl.multiple_of(peer_t[i] * HALF, HALF), HALF)
            dkv_send[i, half, :, 0:2 * DK] = (dkv[half, rows, 0:2 * DK] * scale).astype(BF16)
            dkv_send[i, half, :, 2 * DK:COLS] = dkv[half, rows, 2 * DK:COLS].astype(BF16)
        for cp in home_copies(half):
            cp.start()

    def work(j, d):
        dqp[j, d] = jnp.zeros((2 * HALF, 2 * DK), F32)
        if d == 0:
            @pl.when(low_here(j))
            def _():
                tile(j, 0, 0, z + j, 0)
        else:
            zq = lax.rem(z - j + PLANES, PLANES)
            tile(j, 1, 1, zq, 0)

            @pl.when(j <= z)
            def _():
                tile(j, 1, 1, zq, 1)

    def relay(j, i, last):
        @pl.when(low_here(j))
        def _():
            wait_piece(j, 0, i)

        if last is not True:
            @pl.when(low_here(j) & (z > 0) & jnp.logical_not(last))
            def _():
                for cp in hop_copies(j, 0, i):
                    cp.start()

        wait_piece(j, 1, i)
        if last is not True:
            @pl.when(jnp.logical_not(last))
            def _():
                for cp in hop_copies(j, 1, i):
                    cp.start()

    def pass_sums(j, d, first_hop):
        for i in range(2):
            part = dqp[j, d, piece(i)]
            if not first_hop:
                block = dqr.at[j, d, piece(i)]
                pltpu.make_async_copy(block, block, d_recv.at[j, d, i]).wait()
                part = part + dqr[j, d, piece(i)].astype(F32)
            dqs[j, d, piece(i)] = part.astype(BF16)
            if j is not LAST:
                dq_copy(j, d, i).start()

    for i in range(2):
        for d in range(2):
            wait_piece(1, d, i)

            @pl.when((d == 1) | (low_here(1) & (z > 0)))
            def _():
                for cp in hop_copies(1, d, i):
                    cp.start()
    for i in range(2):
        relay(2, i, False)

    for d in range(2):
        for cp in key_copies()[3 * d:3 * d + 3]:
            cp.wait()
        work(1, d)
        pass_sums(1, d, True)

    for d in range(2):
        dqp[0, d] = jnp.zeros((2 * HALF, 2 * DK), F32)
    tile(0, 0, 0, z, 0)
    tile(0, 0, 1, z, 0)
    tile(0, 0, 1, z, 1)
    their_rows = pl.ds(pl.multiple_of(other * HALF, HALF), HALF)
    for d in range(2):
        loc_send[d] = dqp[0, d, their_rows, :]
    loc_copy = send(loc_send, loc_recv, l_send, l_recv, peers[0])
    loc_copy.start()

    @pl.when(z <= 1)
    def _():
        send_home(1)

    def step(j, carry):
        @pl.when(j > 2)
        def _():
            relay(j, 0, j == LAST)
            relay(j, 1, j == LAST)

        for d in range(2):
            @pl.when(j > 2)
            def _():
                pass_sums(j - 1, d, False)

        for d in range(2):
            work(j, d)

        @pl.when(j == z)
        def _():
            send_home(1)

        return carry

    lax.fori_loop(2, LAST + 1, step, 0)

    def fin_copies(d):
        out = []
        for i, k in enumerate((core, other)):
            rows = pl.ds(pl.multiple_of(k * HALF, HALF), HALF)
            out.append(
                send(dqs.at[LAST, d, rows, :], fin.at[d, core], f_send.at[d, i], f_recv.at[d, i], dev(ring[d], col, k))
            )
        return out

    x_copies = [send(lam_send.at[0], lam_x.at[i], x_send.at[i], x_recv.at[i], peers[i]) for i in range(3)] + [
        pltpu.make_async_remote_copy(
            src_ref=lam_send.at[0], dst_ref=lam_x.at[3 + i], send_sem=x_send.at[3 + i], recv_sem=x_recv.at[3 + i],
            device_id={"seq": to, "head": across}, device_id_type=MESH,
        )
        for i, to in enumerate([me] + peers)
    ]
    z_copies = [
        send(lam_send.at[1], lam_z.at[off - 1], z_send.at[off - 1], z_recv.at[off - 1],
             dev(lax.rem(z + off, PLANES), col, core))
        for off in range(1, PLANES)
    ]
    y_copies = [
        pltpu.make_async_remote_copy(
            src_ref=lam_send.at[2], dst_ref=lam_y.at[i], send_sem=y_send.at[i], recv_sem=y_recv.at[i],
            device_id={"head": to}, device_id_type=MESH,
        )
        for i, to in enumerate(beside)
    ]

    def lam_stage(n):
        if n > 0:
            parts = (x_copies, z_copies)[n - 1]
            for cp in parts:
                cp.wait()
            lam_send[n] = lam_send[n - 1] + jnp.sum((lam_x, lam_z)[n - 1][...], axis=0)
        else:
            lam_send[0] = lam_acc[...]
        for cp in (x_copies, z_copies, y_copies)[n]:
            cp.start()

    lam_stage(0)
    send_home(0)
    lam_stage(1)
    for d in range(2):
        pass_sums(LAST, d, False)
        for cp in fin_copies(d):
            cp.start()
    lam_stage(2)

    key_rows = pl.ds(pl.multiple_of(t_me * HALF, HALF), HALF)
    for half in (1, 0):
        for cp in home_copies(half):
            cp.wait()
        rows = slice(half * HALF, (half + 1) * HALF)
        own = dkv[half, key_rows, :]
        mine_k = own[:, 0:2 * DK] * scale + dkv_recv[1, half, :, 0:2 * DK].astype(F32)
        mine_v = own[:, 2 * DK:COLS] + dkv_recv[1, half, :, 2 * DK:COLS].astype(F32)
        theirs = dkv_recv[0, half].astype(F32) + dkv_recv[2, half].astype(F32)
        for h in range(2):
            val_k = jnp.where(core == h, mine_k, theirs[:, 0:2 * DK]).astype(BF16)
            val_v = jnp.where(core == h, mine_v, theirs[:, 2 * DK:COLS]).astype(BF16)
            dk1_out[rows, h * DK:(h + 1) * DK] = val_k[:, 0:DK]
            dk2_out[rows, h * DK:(h + 1) * DK] = val_k[:, DK:2 * DK]
            dv_out[rows, h * DV:(h + 1) * DV] = val_v

    loc_copy.wait()
    for d in range(2):
        for cp in fin_copies(d):
            cp.wait()
        rows = slice(d * HALF, (d + 1) * HALF)
        mine = dqp[0, d, my_rows, :] + fin[d, core].astype(F32)
        theirs = loc_recv[d] + fin[d, other].astype(F32)
        for h in range(2):
            val = jnp.where(core == h, mine, theirs).astype(BF16)
            dq1_out[rows, h * DK:(h + 1) * DK] = val[:, 0:DK]
            dq2_out[rows, h * DK:(h + 1) * DK] = val[:, DK:2 * DK]

    for cp in y_copies:
        cp.wait()
    total_tile = lam_send[2] + jnp.sum(lam_y[...], axis=0)
    total = -jnp.sum(jnp.sum(total_tile, axis=0, keepdims=True), axis=1, keepdims=True)
    lam_out[0:1, :] = total * e1 * lk1_ref[...]
    lam_out[1:2, :] = total * e1 * lq1_ref[...]
    lam_out[2:3, :] = -total * e2 * lk2_ref[...]
    lam_out[3:4, :] = -total * e2 * lq2_ref[...]

    for cp in first_copies():
        cp.wait_send()
    for j in range(1, LAST):
        for i in range(2):
            @pl.when(low_here(j) & (z > 0))
            def _():
                for cp in hop_copies(j, 0, i):
                    cp.wait_send()

            for cp in hop_copies(j, 1, i):
                cp.wait_send()
            for d in range(2):
                dq_copy(j, d, i).wait_send()


def finish(*refs):
    n = len(refs) // 2
    copies = [pltpu.make_async_copy(refs[i], refs[n + i], refs[-1].at[i]) for i in range(n)]
    for cp in copies:
        cp.start()
    for cp in copies:
        cp.wait()


def fused(*args):
    (q1, q2, k1, k2, v, go, lse1, lse2, d1, d2, starts, skip, lq1, lk1, lq2, lk2) = args
    rows = q1.shape[0]
    vm = pl.BlockSpec(memory_space=pltpu.VMEM)
    hbm = pl.BlockSpec(memory_space=pltpu.HBM)
    dma = pltpu.SemaphoreType.DMA
    lam_tile = (8, 2 * HALF)
    scratch = [
        *[pltpu.VMEM((2, 2 * HALF), F32)] * 4,
        pltpu.VMEM((DEVICES, 2 * HALF), jnp.int32),
        pltpu.SMEM((DEVICES, DEVICES), jnp.int32),
        *[pltpu.VMEM((1, DK), F32)] * 4,
        pltpu.VMEM((2, 2 * HALF, COLS), BF16),
        pltpu.VMEM((2, 8, 2 * HALF), F32),
        pltpu.VMEM((2, 2 * HALF, COLS), BF16),
        pltpu.VMEM((2, PLANE, HALF, COLS), BF16),
        pltpu.VMEM((PLANES, 2, 2 * HALF, COLS), BF16),
        pltpu.VMEM((PLANES, 2, 2, 8, 2 * HALF), F32),
        pltpu.VMEM((PLANES, 2, 2 * HALF, 2 * DK), F32),
        pltpu.VMEM((PLANES, 2, 2 * HALF, 2 * DK), BF16),
        pltpu.VMEM((PLANES, 2, 2 * HALF, 2 * DK), BF16),
        pltpu.VMEM((2, HALF, 2 * DK), F32),
        pltpu.VMEM((2, HALF, 2 * DK), F32),
        pltpu.VMEM((2, 2, HALF, 2 * DK), BF16),
        pltpu.VMEM((2, PLANE * HALF, COLS), F32),
        pltpu.VMEM((3, 2, HALF, COLS), BF16),
        pltpu.VMEM((3, 2, HALF, COLS), BF16),
        pltpu.VMEM(lam_tile, F32),
        pltpu.VMEM((3,) + lam_tile, F32),
        pltpu.VMEM((LAST,) + lam_tile, F32),
        pltpu.VMEM((LAST,) + lam_tile, F32),
        pltpu.VMEM((3,) + lam_tile, F32),
        dma((2, 2, 3)), dma((10,)),
        dma((PLANES, 2, 2)), dma((PLANES, 2, 2)),
        dma((PLANES, 2, 2)), dma((PLANES, 2)),
        dma((4,)), dma((2,)),
        dma((3, 2)), dma((3, 2)),
        dma((PLANES, 2, 2)), dma((PLANES, 2, 2)),
        dma((2, 2)), dma((2, 2)),
        dma, dma,
        dma((3, 2)), dma((3, 2)),
        dma((LAST,)), dma((LAST,)),
        dma((LAST,)), dma((LAST,)),
        dma((3,)), dma((3,)),
    ]
    outs = [jax.ShapeDtypeStruct(a.shape, BF16) for a in (q1, q2, k1, k2, v)]
    outs.append(jax.ShapeDtypeStruct((4, DK), F32))
    row = lambda a: a.reshape(1, DK)
    results = pl.pallas_call(
        kernel,
        out_shape=[pltpu.VMEM(o.shape, o.dtype) for o in outs],
        in_specs=[hbm] * 16,
        out_specs=[vm] * 6,
        scratch_shapes=scratch,
        compiler_params=pltpu.CompilerParams(
            collective_id=0, has_side_effects=True, vmem_limit_bytes=VMEM_LIMIT
        ),
    )(
        q1, q2, go, k1, k2, v, lse1, lse2, d1, d2, starts.reshape(DEVICES, rows), skip,
        row(lq1), row(lk1), row(lq2), row(lk2),
    )
    return pl.pallas_call(
        finish,
        out_shape=outs,
        in_specs=[vm] * 6,
        out_specs=[hbm] * 6,
        scratch_shapes=[dma((6,))],
        compiler_params=pltpu.CompilerParams(vmem_limit_bytes=8 * 1024 * 1024),
    )(*results)


def solution(mesh):
    tok = P("seq", "head")
    stat = P("head", "seq")
    return jax.shard_map(
        fused,
        mesh=mesh,
        in_specs=(tok,) * 6 + (stat,) * 4 + (P(),) * 6,
        out_specs=(tok,) * 5 + (P(),),
        check_vma=False,
    )
```
